32 devices in a mesh: swap: 8 (over z, y), blk: 4 (over x, core).
Axes of the slice: x: 2, y: 2, z: 4, core: 2. Of those that a mesh axis runs over, the one named last changes fastest.
Arguments:
- queries: bfloat16 [4096, 4096], P(('blk', 'swap')), may hold values from -6 to 6
- keys: bfloat16 [4096, 512], P(('blk', 'swap')), may hold values from -6 to 6
- values: bfloat16 [4096, 512], P(('blk', 'swap')), may hold values from -6 to 6
- grad_out: bfloat16 [4096, 4096], P(('blk', 'swap')), may hold values from -6 to 6
- doc_ids: int32 [4096], replicated, may hold values from 0 to 4095, as said below
Outputs:
- grad_queries: bfloat16 [4096, 4096], P(('blk', 'swap'))
- grad_keys: bfloat16 [4096, 512], P(('blk', 'swap'))
- grad_values: bfloat16 [4096, 512], P(('blk', 'swap'))
The draws below stay inside these ranges and needn't reach their ends.
Inputs may be any that keep to these rules, and one draw needn't show every extreme that they name: `doc_ids`: each token's label is the position of the first token of its document, so labels never fall along the sequence; each document holds 1 to 1024 tokens, the last token is a document of its own, and in every draw a document of exactly 1024 tokens ends on the first token of some block of 1024 tokens after the first block.
All inputs are finite; a program needn't handle non-finite values.
Results may differ from the reference program's by a relative error of at most 0.0058.
Values may be sent and summed in bfloat16 or wider, within the bound.
No kernel may reach another device: no remote copies, remote signals or barrier semaphores. Data moves between devices by JAX's collectives and lax.ppermute only.
A program may use at most 64 MiB of HBM per device.

```python
import math
import jax
import jax.numpy as jnp
from jax import lax

HEADS = 32
KV_HEADS = 4
HEAD_DIM = 128
MOST = 1024
SEQ_BLK = 1024
SEQ = 4096


def drawn_start(key):
    blocks_total = SEQ // SEQ_BLK
    chosen = jax.random.randint(jax.random.fold_in(key, 11), (), 1, blocks_total)
    return (chosen * SEQ_BLK - MOST + 1).astype(jnp.int32)


def draw_doc_ids(key, part):
    start = drawn_start(key)
    first_factor = jax.random.randint(jax.random.fold_in(key, 21), (SEQ,), 0, MOST)
    second_factor = jax.random.randint(jax.random.fold_in(key, 22), (SEQ,), 0, MOST)
    lengths = 1 + first_factor * second_factor // MOST
    ends = jnp.cumsum(lengths)
    starts = ends - lengths
    places = jnp.arange(SEQ, dtype=jnp.int32)
    flags = jnp.zeros((SEQ,), jnp.int32).at[starts].set(1, mode='drop')
    inside = (places > start) & (places < start + MOST)
    flags = jnp.where(inside, 0, flags)
    flags = jnp.where((places == start) | (places == start + MOST) | (places == 0) | (places == SEQ - 1), 1, flags)
    labels = jnp.where(flags == 1, places, 0)
    return lax.cummax(labels, axis=0).astype(jnp.int32)


def draw_queries(key, part):
    columns = HEADS * HEAD_DIM
    base_rows = jax.random.normal(jax.random.fold_in(key, 31), (SEQ, columns), jnp.float32)
    return jnp.clip(base_rows, -6.0, 6.0).astype(jnp.bfloat16)


def draw_keys(key, part):
    columns = KV_HEADS * HEAD_DIM
    base_rows = jax.random.normal(jax.random.fold_in(key, 35), (SEQ, columns), jnp.float32)
    return jnp.clip(base_rows, -6.0, 6.0).astype(jnp.bfloat16)


def level_of(key, shape, pieces, low, high):
    gain = 1.0
    for position, blocks in pieces:
        steps = jax.random.uniform(jax.random.fold_in(jax.random.fold_in(key, 6), position), (blocks,), jnp.float32, low / len(pieces), high / len(pieces))
        gain = gain * jnp.repeat(jnp.exp(steps), shape[position] // blocks).reshape((-1,) + (1,) * (len(shape) - 1 - position))
    return gain


def normal_values(rng, dims, scale, limit, cuts=(), kind=jnp.bfloat16):
    values = jax.random.normal(rng, dims, jnp.float32) * scale
    if len(cuts) > 0:
        values = level_of(rng, dims, cuts, -0.22, 0.18) * values
    return jnp.clip(values, min=-limit, max=limit).astype(kind)


def setup_inputs(seed: int = 0) -> dict:
    arg_keys = jax.random.split(jax.random.key(seed), 6)
    return {
        "queries": draw_queries(jax.random.fold_in(arg_keys[5], 71), 0),
        "keys": draw_keys(jax.random.fold_in(arg_keys[5], 71), 0),
        "values": normal_values(arg_keys[2], (SEQ, KV_HEADS * HEAD_DIM), 1.0, 6.0, ((0, 32),)),
        "grad_out": normal_values(arg_keys[3], (SEQ, HEADS * HEAD_DIM), 1.0, 6.0, ((0, 32),)),
        "doc_ids": draw_doc_ids(jax.random.fold_in(arg_keys[5], 71), 0),
    }


masked_value = -1e+30

def reference(queries, keys, values, grad_out, doc_ids):
    inv_root = 1.0 / math.sqrt(HEAD_DIM)
    group_size = HEADS // KV_HEADS
    tile_rows = min(512, SEQ)
    key_width = MOST + tile_rows
    tile_count = SEQ // tile_rows
    q_four = queries.reshape(SEQ, KV_HEADS, group_size, HEAD_DIM)
    g_four = grad_out.reshape(SEQ, KV_HEADS, group_size, HEAD_DIM)
    k_padded = jnp.concatenate([jnp.zeros((MOST, KV_HEADS * HEAD_DIM), keys.dtype), keys], 0).reshape(MOST + SEQ, KV_HEADS, HEAD_DIM)
    v_padded = jnp.concatenate([jnp.zeros((MOST, KV_HEADS * HEAD_DIM), values.dtype), values], 0).reshape(MOST + SEQ, KV_HEADS, HEAD_DIM)
    doc_padded = jnp.concatenate([jnp.full((MOST,), -1, jnp.int32), doc_ids.astype(jnp.int32)], 0)

    def one_tile(running, step_index):
        dk_acc, dv_acc = running
        tile_start = (step_index * tile_rows).astype(jnp.int32)
        q_tile = lax.dynamic_slice_in_dim(q_four, tile_start, tile_rows, 0).astype(jnp.float32)
        g_tile = lax.dynamic_slice_in_dim(g_four, tile_start, tile_rows, 0).astype(jnp.float32)
        k_tile = lax.dynamic_slice_in_dim(k_padded, tile_start, key_width, 0).astype(jnp.float32)
        v_tile = lax.dynamic_slice_in_dim(v_padded, tile_start, key_width, 0).astype(jnp.float32)
        q_docs = lax.dynamic_slice_in_dim(doc_ids.astype(jnp.int32), tile_start, tile_rows, 0)
        k_docs = lax.dynamic_slice_in_dim(doc_padded, tile_start, key_width, 0)
        q_place = jnp.arange(tile_rows, dtype=jnp.int32)
        k_place = jnp.arange(key_width, dtype=jnp.int32) - MOST
        allowed = (k_place[None, :] <= q_place[:, None]) & (k_docs[None, :] == q_docs[:, None])
        scores = jnp.einsum('qgrd,kgd->grqk', q_tile, k_tile) * inv_root
        scores = jnp.where(allowed, scores, masked_value)
        row_max = lax.optimization_barrier(jnp.max(scores, axis=-1, keepdims=True))
        raised = jnp.exp(scores - row_max)
        weights = raised / lax.optimization_barrier(jnp.sum(raised, axis=-1, keepdims=True))
        weights_f = lax.optimization_barrier(weights.astype(jnp.bfloat16)).astype(jnp.float32)
        attended = jnp.einsum('grqk,kgd->qgrd', weights_f, v_tile)
        row_dot = jnp.transpose(lax.optimization_barrier(jnp.sum(g_tile * attended, axis=-1)), (1, 2, 0))
        dweights = jnp.einsum('qgrd,kgd->grqk', g_tile, v_tile)
        d_scores = weights * (dweights - row_dot[..., None])
        d_scores = lax.optimization_barrier(d_scores.astype(jnp.bfloat16)).astype(jnp.float32)
        dq_tile = (jnp.einsum('grqk,kgd->qgrd', d_scores, k_tile) * inv_root).astype(jnp.bfloat16)
        dk_tile = jnp.einsum('grqk,qgrd->kgd', d_scores, q_tile) * inv_root
        dv_tile = jnp.einsum('grqk,qgrd->kgd', weights_f, g_tile)
        dk_acc = lax.dynamic_update_slice_in_dim(dk_acc, lax.dynamic_slice_in_dim(dk_acc, tile_start, key_width, 0) + dk_tile, tile_start, 0)
        dv_acc = lax.dynamic_update_slice_in_dim(dv_acc, lax.dynamic_slice_in_dim(dv_acc, tile_start, key_width, 0) + dv_tile, tile_start, 0)
        return ((dk_acc, dv_acc), dq_tile)
    zero_acc = jnp.zeros((MOST + SEQ, KV_HEADS, HEAD_DIM), jnp.float32)
    (dk_acc, dv_acc), dq_tiles = lax.scan(one_tile, (zero_acc, zero_acc), jnp.arange(tile_count, dtype=jnp.int32))
    grad_queries = dq_tiles.reshape(SEQ, HEADS * HEAD_DIM)
    grad_keys = dk_acc[MOST:].reshape(SEQ, KV_HEADS * HEAD_DIM).astype(jnp.bfloat16)
    grad_values = dv_acc[MOST:].reshape(SEQ, KV_HEADS * HEAD_DIM).astype(jnp.bfloat16)
    return (grad_queries, grad_keys, grad_values)
```

```python
import functools
import math

import jax
import jax.numpy as jnp
from jax import lax
from jax.experimental import pallas as pl
from jax.experimental.pallas import tpu as pltpu
from jax.sharding import PartitionSpec as P

HEAD_DIM = 128
MOST = 1024
BF16 = jnp.bfloat16
F32 = jnp.float32
LOG2E = 1.4426950408889634
MIB = 1024 * 1024

NN = (((1,), (0,)), ((), ()))
NT = (((1,), (1,)), ((), ()))
TN = (((0,), (0,)), ((), ()))


def dot(a, b, dims):
    return lax.dot_general(a, b, dims, preferred_element_type=F32)


def vmem_call(kernel, out_shapes, args, scratch=(), hbm=(), smem=(), after=(), through=(), mib=8, flops=0, name=None):
    def space(i):
        return pltpu.SMEM if i in smem else pl.ANY if i in hbm else pltpu.VMEM

    specs = [pl.BlockSpec(memory_space=space(i)) for i in range(len(args))]
    specs += [pl.BlockSpec(memory_space=pl.ANY)] * (len(after) + len(through))
    outs = [pl.BlockSpec(memory_space=pltpu.VMEM)] * len(out_shapes)
    outs += [pl.BlockSpec(memory_space=pl.ANY)] * len(through)
    n_args, n_out = len(args), len(out_shapes)
    n_in, n_made = len(specs), len(outs)

    def run(*refs):
        kernel(*refs[:n_args], *refs[n_in : n_in + n_out], *refs[n_in + n_made :])

    return pl.pallas_call(
        run,
        out_shape=list(out_shapes) + [jax.ShapeDtypeStruct(t.shape, t.dtype) for t in through],
        in_specs=specs,
        out_specs=outs,
        input_output_aliases={n_args + len(after) + i: n_out + i for i in range(len(through))},
        scratch_shapes=list(scratch),
        compiler_params=pltpu.CompilerParams(vmem_limit_bytes=mib * MIB),
        cost_estimate=pl.CostEstimate(flops=flops, bytes_accessed=0, transcendentals=0),
        name=name,
    )(*args, *after, *through)


def place():
    blk, swap = lax.axis_index("blk"), lax.axis_index("swap")
    return lax.rem(blk, 2), lax.rem(swap, 2), lax.div(swap, 2)


def quarters():
    core, y, _ = place()
    return [2 * core + y, 2 * (1 - core) + y, 2 * core + 1 - y, 2 * (1 - core) + 1 - y]


def split_kernel(a_ref, b_ref, *rest):
    outs, sems = rest[:-1], rest[-1]
    width = a_ref.shape[1] // 4
    copies = []
    for quarter, out in zip(quarters(), outs):
        columns = pl.ds(pl.multiple_of(quarter * width, 128), width)
        for src, place_out in ((a_ref, slice(0, width)), (b_ref, slice(width, 2 * width))):
            copies.append(
                pltpu.make_async_copy(src.at[:, columns], out.at[:, place_out], sems.at[len(copies)])
            )
    for copy in copies:
        copy.start()
    for copy in copies:
        copy.wait()


def select_chunks(blocks, own, by_core, by_y, by_diag):
    core, y, _ = place()
    rows = own.shape[0]
    here = pl.ds(pl.multiple_of(y * rows, rows), rows)
    there = pl.ds(pl.multiple_of((1 - y) * rows, rows), rows)
    for c in (0, 1):

        @pl.when(core == c)
        def _(c=c):
            blocks[c][here, :] = own[...]
            blocks[c][there, :] = by_y[...]
            blocks[1 - c][here, :] = by_core[...]
            blocks[1 - c][there, :] = by_diag[...]


def fill_payloads(n_out, up, down, outs):
    _, _, z = place()
    for k, out in enumerate(outs, 1):

        @pl.when(z + k < n_out)
        def _(out=out):
            out[...] = up[...]

        @pl.when(z + k >= n_out)
        def _(out=out):
            out[...] = down[...]


def first_payload_kernel(n_out, own, by_core, by_y, by_diag, even, odd, *outs):
    select_chunks((even, odd), own, by_core, by_y, by_diag)
    fill_payloads(n_out, odd, even, outs)


def second_payload_kernel(n_out, even, rim, *outs):
    fill_payloads(n_out, even, rim, outs)


def attend_kernel(odd, second, n_slots, seq_blk, own, by_core, by_y, by_diag, starts, doc_scalars, *rest):
    slots, rest = rest[:n_slots], rest[n_slots:]
    if second:
        dq_first, dq_outs, rest = rest[0], rest[1:5], rest[5:]
        rest, dq_out = rest[:-1], rest[-1]
    else:
        dq_out, rest = rest[0], rest[1:]
    sums, rest = rest[:n_slots], rest[n_slots:]
    q_rows, g_rows, q_cols, g_cols, kv, scores, dweights, dq_cols, acc = rest
    core, y, z = place()
    tok = own.shape[0]
    width = own.shape[1] // 2
    heads = width // HEAD_DIM
    pair = 2 * tok
    window = (n_slots - 1) * pair
    inv_root = 1.0 / math.sqrt(HEAD_DIM)
    scale = inv_root * LOG2E
    block = 2 * lax.div(lax.axis_index("blk"), 2) + odd
    pair_start = block * seq_blk + z * pair

    def stack(unit, src):
        for h in range(heads):
            rows = slice(h * tok, (h + 1) * tok)
            cols = slice(h * HEAD_DIM, (h + 1) * HEAD_DIM)
            q_rows[unit, rows, :] = src[:, cols]
            g_rows[unit, rows, :] = src[:, width + h * HEAD_DIM : width + (h + 1) * HEAD_DIM]

    @pl.when(core == odd)
    def _():
        stack(y, own)
        stack(1 - y, by_y)

    @pl.when(core != odd)
    def _():
        stack(y, by_core)
        stack(1 - y, by_diag)

    for i, slot in enumerate(slots):
        kv[i * pair : (i + 1) * pair, :] = slot[...]
    acc[...] = jnp.zeros_like(acc)

    for unit in (0, 1):
        first = pair_start + unit * tok
        base = first - window
        lo = starts[pl.ds(lax.div(first, 128), 1), :]
        t = lax.broadcasted_iota(jnp.int32, (1, tok), 1)
        key_place = lax.broadcasted_iota(jnp.int32, (tok, tok), 0)
        begin = lax.div(doc_scalars[first] - base, tok)
        count = window // tok + 1

        q_cols[...] = q_rows[unit].T
        g_cols[...] = g_rows[unit].T

        def key_rows(j):
            return pl.ds(pl.multiple_of(j * tok + unit * tok, tok), tok)

        def own_rows(j):
            return pl.ds(pl.multiple_of(j * tok, tok), tok)

        def score_step(j, top):
            place_j = key_place + (base + j * tok)
            allowed = (place_j >= lo) & (place_j <= t + first)
            bias = jnp.where(allowed, 0.0, -1e30).astype(F32)
            s = dot(kv[key_rows(j), :HEAD_DIM], q_cols[...], NN)
            s = s + jnp.concatenate([bias] * heads, axis=1)
            scores[own_rows(j), :] = s
            return jnp.maximum(top, jnp.max(s, axis=0, keepdims=True))

        top = lax.fori_loop(begin, count, score_step, jnp.full((1, heads * tok), -3e38, F32))

        def weight_step(j, running):
            total, rowdot = running
            p = jnp.exp2((scores[own_rows(j), :] - top) * scale)
            d = dot(kv[key_rows(j), HEAD_DIM:], g_cols[...], NN)
            scores[own_rows(j), :] = p
            dweights[own_rows(j), :] = d
            return (
                total + jnp.sum(p, axis=0, keepdims=True),
                rowdot + jnp.sum(p * d, axis=0, keepdims=True),
            )

        zero = jnp.zeros((1, heads * tok), F32)
        total, rowdot = lax.fori_loop(begin, count, weight_step, (zero, zero))
        inv_total = 1.0 / total
        rowdot = rowdot * inv_total
        dq_cols[...] = jnp.zeros_like(dq_cols)

        def grad_step(j, carry):
            w = scores[own_rows(j), :] * inv_total
            ds = (w * (dweights[own_rows(j), :] - rowdot)).astype(BF16)
            rows = key_rows(j)
            acc[rows, :HEAD_DIM] += dot(ds, q_rows[unit], NN)
            acc[rows, HEAD_DIM:] += dot(w.astype(BF16), g_rows[unit], NN)
            dq_cols[...] += dot(kv[rows, :HEAD_DIM], ds, TN)
            return carry

        lax.fori_loop(begin, count, grad_step, 0)
        dq = (dq_cols[...] * inv_root).T
        for h in range(heads):
            dq_out[unit * tok : (unit + 1) * tok, h * HEAD_DIM : (h + 1) * HEAD_DIM] = dq[
                h * tok : (h + 1) * tok, :
            ].astype(BF16)

    for i, out in enumerate(sums):
        rows = slice(i * pair, (i + 1) * pair)
        out[:, :HEAD_DIM] = (acc[rows, :HEAD_DIM] * inv_root).astype(out.dtype)
        out[:, HEAD_DIM:] = acc[rows, HEAD_DIM:].astype(out.dtype)

    if second:
        for out, c, yy in zip(dq_outs, (core, 1 - core, core, 1 - core), (y, y, 1 - y, 1 - y)):
            chunk = pl.ds(pl.multiple_of(yy * tok, tok), tok)

            @pl.when(c == odd)
            def _(out=out, chunk=chunk):
                out[...] = dq_out[chunk, :]

            @pl.when(c != odd)
            def _(out=out, chunk=chunk):
                out[...] = dq_first[chunk, :]


def add_terms(n_out, up, down, terms):
    _, _, z = place()
    for k, term in enumerate(terms, 1):
        value = term[...].astype(F32)
        wrapped = (z + k >= n_out).astype(F32)
        up = up + value * (1.0 - wrapped)
        down = down + value * wrapped
    return up, down


def even_sum_kernel(n_out, n_terms, own_up, *refs):
    terms, own_down, up_out, down_out = refs[:n_terms], refs[n_terms:-2], refs[-2], refs[-1]
    down = own_down[0][...] if own_down else jnp.zeros(up_out.shape, F32)
    up, down = add_terms(n_out, own_up[...], down, terms)
    up_out[...] = up
    down_out[...] = down.astype(down_out.dtype)


def home_kernel(n_out, n_terms, odd_up, even_total, rim, *refs):
    terms, refs = refs[:n_terms], refs[n_terms:]
    own_down, outs, total = refs[:-5], refs[-5:-1], refs[-1]
    tok = odd_up.shape[0] // 2
    down = own_down[0][...] if own_down else jnp.zeros(odd_up.shape, F32)
    up, down = add_terms(n_out, odd_up[...], down, terms)
    total[0] = even_total[...] + down
    total[1] = up + rim[...].astype(F32)
    core, y, _ = place()
    for out, c, yy in zip(outs, (core, 1 - core, core, 1 - core), (y, y, 1 - y, 1 - y)):
        out[...] = total[c, pl.ds(pl.multiple_of(yy * tok, tok), tok), :].astype(out.dtype)


def finish_kernel(*refs):
    dq, kv, (q_out, k_out, v_out) = refs[:4], refs[4:8], refs[8:]
    q_width = dq[0].shape[1]
    kv_width = kv[0].shape[1] // 2
    for quarter, dq_part, kv_part in zip(quarters(), dq, kv):
        q_out[:, pl.ds(pl.multiple_of(quarter * q_width, 128), q_width)] = dq_part[...]
        columns = pl.ds(pl.multiple_of(quarter * kv_width, 128), kv_width)
        k_out[:, columns] = kv_part[:, :kv_width].astype(BF16)
        v_out[:, columns] = kv_part[:, kv_width:].astype(BF16)


def body(queries, keys, values, grad_out, doc_ids):
    tok = queries.shape[0]
    n_blk, n_swap = lax.axis_size("blk"), lax.axis_size("swap")
    n_out = n_swap // 2
    seq_blk = tok * n_swap
    pair = 2 * tok
    far = -(-MOST // pair)
    q_width, kv_width = queries.shape[1] // 4, keys.shape[1] // 4
    both = ("swap", "blk")
    devices = [(b, s) for b in range(n_blk) for s in range(n_swap)]

    def index(b, s):
        return s * n_blk + b

    routes = [
        [(index(b, s), index(b ^ 1, s)) for b, s in devices],
        [(index(b, s), index(b, s ^ 1)) for b, s in devices],
        [(index(b, s), index(b ^ 1, s ^ 1)) for b, s in devices],
    ]

    def to_partners(parts):
        return [lax.ppermute(part, both, route) for part, route in zip(parts, routes)]

    def along_z(part, k):
        route = [(s, 2 * ((s // 2 + k) % n_out) + s % 2) for s in range(n_swap)]
        return lax.ppermute(part, "swap", route)

    def along_x(part, step):
        return lax.ppermute(
            part, "blk", [(b, b + step) for b in range(n_blk) if 0 <= b + step < n_blk]
        )

    def shape(rows, cols, dtype=BF16):
        return jax.ShapeDtypeStruct((rows, cols), dtype)

    def split(a, b, width, name):
        return vmem_call(
            split_kernel,
            [shape(tok, 2 * width)] * 4,
            (a, b),
            scratch=[pltpu.SemaphoreType.DMA((8,))],
            hbm=(0, 1),
            name=name,
        )

    kv_parts = split(keys, values, kv_width, "split_kv")
    kv_recv = to_partners(kv_parts[1:])
    qg_parts = split(queries, grad_out, q_width, "split_qg")

    block_shape = shape(pair, 2 * kv_width)
    shifts = [k for k in range(1, far + 1) if k < n_out]
    made = vmem_call(
        functools.partial(first_payload_kernel, n_out),
        [block_shape] * (2 + len(shifts)),
        (kv_parts[0], *kv_recv),
        through=qg_parts,
        name="payload_odd",
    )
    even, odd, odd_pay, qg_parts = made[0], made[1], made[2:-4], made[-4:]
    rim = along_x(odd, 2)
    odd_got = [along_z(part, k) for k, part in zip(shifts, odd_pay)]
    qg_recv = to_partners(qg_parts[1:])
    even_pay = vmem_call(
        functools.partial(second_payload_kernel, n_out),
        [block_shape] * len(shifts),
        (even, rim),
        name="payload_even",
    )
    even_got = [along_z(part, k) for k, part in zip(shifts, even_pay)]

    starts = doc_ids.reshape(-1, 128)
    n_slots = far + 1
    rows = (q_width // HEAD_DIM) * tok
    sum_dtypes = [F32 if (i == far or far - i == n_out) else BF16 for i in range(n_slots)]
    sum_shapes = [shape(pair, 2 * kv_width, dtype) for dtype in sum_dtypes]

    def attend(which, slots, dq_first=None):
        second = dq_first is not None
        dq_shapes = [shape(tok, q_width)] * 4 if second else [shape(pair, q_width)]
        return vmem_call(
            functools.partial(attend_kernel, which, second, n_slots, seq_blk),
            dq_shapes + sum_shapes,
            (qg_parts[0], *qg_recv, starts, doc_ids, *slots) + ((dq_first,) if second else ()),
            scratch=[
                pltpu.VMEM((2, rows, HEAD_DIM), BF16),
                pltpu.VMEM((2, rows, HEAD_DIM), BF16),
                pltpu.VMEM((HEAD_DIM, rows), BF16),
                pltpu.VMEM((HEAD_DIM, rows), BF16),
                pltpu.VMEM((n_slots * pair, 2 * kv_width), BF16),
                pltpu.VMEM((MOST + tok, rows), F32),
                pltpu.VMEM((MOST + tok, rows), F32),
                pltpu.VMEM((HEAD_DIM, rows), F32),
                pltpu.VMEM((n_slots * pair, 2 * kv_width), F32),
            ]
            + ([pltpu.VMEM((pair, q_width), BF16)] if second else []),
            smem=(5,),
            mib=24,
            flops=6_000_000_000,
            name="attend_odd" if which else "attend_even",
        )

    def slots_of(up, down, got):
        return [down if k == n_out else got[k - 1] for k in range(far, 0, -1)] + [up]

    def sent(sums):
        return [sums[far - k] for k in shifts]

    def own_down(sums):
        return [sums[0]] if far == n_out else []

    def back_along_z(parts):
        return [along_z(part, n_out - k) for k, part in zip(shifts, parts)]

    dq_even, *even_sums = attend(0, slots_of(even, rim, even_got))
    even_back = back_along_z(sent(even_sums))
    made = attend(1, slots_of(odd, even, odd_got), dq_even)
    dq_parts, odd_sums = made[:4], made[4:]
    dq_recv = to_partners(dq_parts[1:])
    even_total, rim_total, *odd_sent = vmem_call(
        functools.partial(even_sum_kernel, n_out, len(shifts)),
        [shape(pair, 2 * kv_width, F32), block_shape],
        (even_sums[far], *even_back, *own_down(even_sums)),
        through=sent(odd_sums),
        name="even_sum",
    )
    rim_home = along_x(rim_total, -2)
    odd_back = back_along_z(odd_sent)
    home = vmem_call(
        functools.partial(home_kernel, n_out, len(shifts)),
        [shape(tok, 2 * kv_width, F32)] + [shape(tok, 2 * kv_width)] * 3,
        (odd_sums[far], even_total, rim_home, *odd_back, *own_down(odd_sums)),
        scratch=[pltpu.VMEM((2, pair, 2 * kv_width), F32)],
        name="home",
    )
    kv_home = to_partners(home[1:])
    return vmem_call(
        finish_kernel,
        [shape(*queries.shape), shape(*keys.shape), shape(*values.shape)],
        (dq_parts[0], *dq_recv, home[0], *kv_home),
        name="finish",
    )


def solution(mesh):
    spec = P(("blk", "swap"), None)
    return jax.shard_map(
        lambda *args: tuple(body(*args)),
        mesh=mesh,
        in_specs=(spec, spec, spec, spec, P()),
        out_specs=(spec, spec, spec),
        check_vma=False,
    )
```

```python
import functools
import math

import jax
import jax.numpy as jnp
from jax import lax
from jax.experimental import pallas as pl
from jax.experimental.pallas import tpu as pltpu
from jax.sharding import PartitionSpec as P

HEAD_DIM = 128
MOST = 1024
BF16 = jnp.bfloat16
F32 = jnp.float32
LOG2E = 1.4426950408889634
MIB = 1024 * 1024

NN = (((1,), (0,)), ((), ()))
NT = (((1,), (1,)), ((), ()))
TN = (((0,), (0,)), ((), ()))


def dot(a, b, dims):
    return lax.dot_general(a, b, dims, preferred_element_type=F32)


def vmem_call(kernel, out_shapes, args, scratch=(), hbm=(), smem=(), after=(), through=(), mib=8, flops=0, name=None):
    def space(i):
        return pltpu.SMEM if i in smem else pltpu.HBM if i in hbm else pltpu.VMEM

    specs = [pl.BlockSpec(memory_space=space(i)) for i in range(len(args))]
    specs += [pl.BlockSpec(memory_space=pl.ANY)] * (len(after) + len(through))
    outs = [pl.BlockSpec(memory_space=pltpu.VMEM)] * len(out_shapes)
    outs += [pl.BlockSpec(memory_space=pl.ANY)] * len(through)
    n_args, n_out = len(args), len(out_shapes)
    n_in, n_made = len(specs), len(outs)

    def run(*refs):
        kernel(*refs[:n_args], *refs[n_in : n_in + n_out], *refs[n_in + n_made :])

    return pl.pallas_call(
        run,
        out_shape=list(out_shapes) + [jax.ShapeDtypeStruct(t.shape, t.dtype) for t in through],
        in_specs=specs,
        out_specs=outs,
        input_output_aliases={n_args + len(after) + i: n_out + i for i in range(len(through))},
        scratch_shapes=list(scratch),
        compiler_params=pltpu.CompilerParams(vmem_limit_bytes=mib * MIB),
        cost_estimate=pl.CostEstimate(flops=flops, bytes_accessed=0, transcendentals=0),
        name=name,
    )(*args, *after, *through)


def place():
    blk, swap = lax.axis_index("blk"), lax.axis_index("swap")
    return lax.rem(blk, 2), lax.rem(swap, 2), lax.div(swap, 2)


def quarters():
    core, y, _ = place()
    return [2 * core + y, 2 * (1 - core) + y, 2 * core + 1 - y, 2 * (1 - core) + 1 - y]


def split_kernel(groups, a_ref, b_ref, *rest):
    outs, sems = rest[:-1], rest[-1]
    width = a_ref.shape[1] // 4
    numbers = quarters()
    copies = []
    for group, out in zip(groups, outs):
        for i, member in enumerate(group(numbers)):
            columns = pl.ds(pl.multiple_of(member * width, 128), width)
            for j, src in enumerate((a_ref, b_ref)):
                dst = out.at[:, (2 * i + j) * width : (2 * i + j + 1) * width]
                copies.append(pltpu.make_async_copy(src.at[:, columns], dst, sems.at[len(copies)]))
    for copy in copies:
        copy.start()
    for copy in copies:
        copy.wait()


def choose_kernel(mine, got, *outs):
    core, y, _ = place()
    width = mine.shape[1] // 2
    for odd, (keep, send) in zip((1, 0), (outs[:2], outs[2:])):
        for out, yy in ((keep, y), (send, 1 - y)):
            columns = pl.ds(pl.multiple_of(yy * width, 128), width)

            @pl.when(core == odd)
            def _(out=out, columns=columns):
                out[...] = mine[:, columns]

            @pl.when(core != odd)
            def _(out=out, columns=columns):
                out[...] = got[:, columns]


def select_chunks(blocks, own, by_core, by_y, by_diag):
    core, y, _ = place()
    rows = own.shape[0]
    here = pl.ds(pl.multiple_of(y * rows, rows), rows)
    there = pl.ds(pl.multiple_of((1 - y) * rows, rows), rows)
    for c in (0, 1):

        @pl.when(core == c)
        def _(c=c):
            blocks[c][here, :] = own[...]
            blocks[c][there, :] = by_y[...]
            blocks[1 - c][here, :] = by_core[...]
            blocks[1 - c][there, :] = by_diag[...]


def fill_payloads(n_out, up, down, outs):
    _, _, z = place()
    for k, out in enumerate(outs, 1):

        @pl.when(z + k < n_out)
        def _(out=out):
            out[...] = up[...]

        @pl.when(z + k >= n_out)
        def _(out=out):
            out[...] = down[...]


def payload_kernel(n_out, n_shifts, own, by_core, by_y, by_diag, even, odd, *outs):
    select_chunks((even, odd), own, by_core, by_y, by_diag)
    fill_payloads(n_out, odd, even, outs[:n_shifts])
    fill_payloads(n_out, even, odd, outs[n_shifts:])


def attend_kernel(odd, n_slots, seq_blk, keep, by_y, starts, doc_scalars, *rest):
    slots, rest = rest[:n_slots], rest[n_slots:]
    dq_keep, dq_send, rest = rest[0], rest[1], rest[2:]
    sums, rest = rest[:n_slots], rest[n_slots:]
    q_rows, g_rows, keys, vals, scores, dweights, dq_cols, acc, stats, dq_both = rest
    _, y, z = place()
    tok = keep.shape[0]
    width = keep.shape[1] // 2
    heads = width // HEAD_DIM
    pair = 2 * tok
    window = (n_slots - 1) * pair
    inv_root = 1.0 / math.sqrt(HEAD_DIM)
    scale = inv_root * LOG2E
    block = 2 * lax.div(lax.axis_index("blk"), 2) + odd
    first = block * seq_blk + z * pair
    base = first - window
    step_cols = 2 * tok
    n_steps = 2 * width // step_cols

    def stack(unit, src):
        for h in range(heads):
            rows = pl.ds(pl.multiple_of(unit * width + h * tok, tok), tok)
            q_rows[rows, :HEAD_DIM] = src[:, h * HEAD_DIM : (h + 1) * HEAD_DIM]
            g_rows[rows, :] = src[:, width + h * HEAD_DIM : width + (h + 1) * HEAD_DIM]

    stack(y, keep)
    stack(1 - y, by_y)
    unity = (
        lax.broadcasted_iota(jnp.int32, (tok, tok), 0) == lax.broadcasted_iota(jnp.int32, (tok, tok), 1)
    )
    unity = jnp.where(unity, 1.0, 0.0).astype(BF16)
    for h in range(2 * heads):
        rows = slice(h * tok, (h + 1) * tok)
        q_rows[rows, HEAD_DIM:] = unity
    for i, slot in enumerate(slots):
        rows = slice(i * pair, (i + 1) * pair)
        for unit in (0, 1):
            keys[unit, rows, :HEAD_DIM] = slot[:, :HEAD_DIM]
        vals[rows, :] = slot[:, HEAD_DIM:]

    begin = lax.div(doc_scalars[first] - base, pair)

    def rows_of(j):
        return pl.ds(pl.multiple_of(j * pair, pair), pair)

    def cols_of(n):
        return slice(n * step_cols, (n + 1) * step_cols)

    def unit_of(n):
        return n * step_cols // width

    def fold(op, x):
        return op(x.reshape(x.shape[0] // 8, 8, x.shape[1]), axis=0)

    stats[0] = jnp.full(stats.shape[1:], -3e38, F32)
    stats[1] = jnp.zeros(stats.shape[1:], F32)
    stats[2] = jnp.zeros(stats.shape[1:], F32)
    dq_cols[...] = jnp.zeros_like(dq_cols)
    t = lax.broadcasted_iota(jnp.int32, (1, tok), 1)
    key_place = lax.broadcasted_iota(jnp.int32, (pair, tok), 0)
    lows = [starts[pl.ds(lax.div(first, 128) + unit, 1), :] for unit in (0, 1)]

    def score_step(j, carry):
        place_j = key_place + (base + j * pair)
        for unit in (0, 1):
            allowed = (place_j >= lows[unit]) & (place_j <= t + (first + unit * tok))
            keys[unit, rows_of(j), HEAD_DIM:] = jnp.where(allowed, 0.0, -1e30).astype(BF16)
        for n in range(n_steps):
            s = dot(keys[unit_of(n), rows_of(j), :], q_rows[cols_of(n), :], NT)
            scores[rows_of(j), cols_of(n)] = s
            stats[0, :, cols_of(n)] = jnp.maximum(stats[0, :, cols_of(n)], fold(jnp.max, s))
        return carry

    lax.fori_loop(begin, n_slots, score_step, 0)
    for n in range(n_steps):
        top = jnp.max(stats[0, :, cols_of(n)], axis=0, keepdims=True)
        stats[0, :, cols_of(n)] = jnp.broadcast_to(top, (8, step_cols))

    def weight_step(j, carry):
        for n in range(n_steps):
            p = jnp.exp2((scores[rows_of(j), cols_of(n)] - stats[0, 0:1, cols_of(n)]) * scale)
            scores[rows_of(j), cols_of(n)] = p
            stats[1, :, cols_of(n)] += fold(jnp.sum, p)
            dweights[rows_of(j), cols_of(n)] = dot(vals[rows_of(j), :], g_rows[cols_of(n), :], NT)
        return carry

    lax.fori_loop(begin, n_slots, weight_step, 0)
    for n in range(n_steps):
        inv = 1.0 / jnp.sum(stats[1, :, cols_of(n)], axis=0, keepdims=True)
        stats[1, :, cols_of(n)] = jnp.broadcast_to(inv, (8, step_cols))

    def value_step(j, carry):
        total = jnp.zeros((pair, HEAD_DIM), F32)
        for n in range(n_steps):
            d = dweights[rows_of(j), cols_of(n)]
            w = scores[rows_of(j), cols_of(n)] * stats[1, 0:1, cols_of(n)]
            wb = w.astype(BF16)
            total = total + dot(wb, g_rows[cols_of(n), :], NN)
            scores[rows_of(j), cols_of(n)] = w
            stats[2, :, cols_of(n)] += fold(jnp.sum, wb.astype(F32) * d)
        acc[rows_of(j), HEAD_DIM:] = total
        return carry

    lax.fori_loop(begin, n_slots, value_step, 0)
    for n in range(n_steps):
        rowdot = jnp.sum(stats[2, :, cols_of(n)], axis=0, keepdims=True)
        stats[2, :, cols_of(n)] = jnp.broadcast_to(rowdot, (8, step_cols))

    def grad_step(j, carry):
        total = jnp.zeros((pair, HEAD_DIM), F32)
        k_cols = keys[0, rows_of(j), :HEAD_DIM].T
        for n in range(n_steps):
            rest = dweights[rows_of(j), cols_of(n)] - stats[2, 0:1, cols_of(n)]
            ds = (scores[rows_of(j), cols_of(n)] * rest).astype(BF16)
            total = total + dot(ds, q_rows[cols_of(n), :HEAD_DIM], NN)
            dq_cols[:, cols_of(n)] += dot(k_cols, ds, NN)
        acc[rows_of(j), :HEAD_DIM] = total * inv_root
        return carry

    lax.fori_loop(begin, n_slots, grad_step, 0)

    for h in range(2 * heads):
        unit, head = h // heads, h % heads
        dq = (dq_cols[:, h * tok : (h + 1) * tok] * inv_root).T
        dq_both[unit, :, head * HEAD_DIM : (head + 1) * HEAD_DIM] = dq.astype(BF16)
    dq_keep[...] = dq_both[y]
    dq_send[...] = dq_both[1 - y]

    for i, out in enumerate(sums):

        @pl.when(i >= begin)
        def _(i=i, out=out):
            out[...] = acc[i * pair : (i + 1) * pair, :].astype(out.dtype)

        @pl.when(i < begin)
        def _(out=out):
            out[...] = jnp.zeros_like(out)


def add_terms(n_out, up, down, terms):
    _, _, z = place()
    for k, term in enumerate(terms, 1):
        value = term[...].astype(F32)
        wrapped = (z + k >= n_out).astype(F32)
        up = up + value * (1.0 - wrapped)
        down = down + value * wrapped
    return up, down


def odd_sum_kernel(n_out, n_terms, own_odd, *refs):
    terms, own_even, (odd_out, even_out) = refs[:n_terms], refs[n_terms:-2], refs[-2:]
    even = own_even[0][...] if own_even else jnp.zeros(even_out.shape, F32)
    odd_out[...], even_out[...] = add_terms(n_out, own_odd[...], even, terms)


def home_kernel(n_out, n_terms, own_even, odd_total, even_total, *refs):
    terms, refs = refs[:n_terms], refs[n_terms:]
    rim, outs, total = refs[:-5], refs[-5:-1], refs[-1]
    tok = own_even.shape[0] // 2
    odd = odd_total[...]
    if rim:
        odd = odd + rim[0][...].astype(F32)
    total[0], total[1] = add_terms(n_out, own_even[...] + even_total[...], odd, terms)
    core, y, _ = place()
    for out, c, yy in zip(outs, (core, 1 - core, core, 1 - core), (y, y, 1 - y, 1 - y)):
        out[...] = total[c, pl.ds(pl.multiple_of(yy * tok, tok), tok), :].astype(out.dtype)


def cross_kernel(odd_keep, odd_got, even_keep, even_got, out):
    core, y, _ = place()
    width = odd_keep.shape[1]
    for c, keep, got in ((0, odd_keep, odd_got), (1, even_keep, even_got)):

        @pl.when(core == c)
        def _(keep=keep, got=got):
            out[:, pl.ds(pl.multiple_of(y * width, 128), width)] = keep[...]
            out[:, pl.ds(pl.multiple_of((1 - y) * width, 128), width)] = got[...]


def finish_kernel(odd_keep, odd_got, even_keep, even_got, crossed, *refs):
    parts, (out, k_out, v_out) = refs[:4], refs[4:]
    core, y, _ = place()
    width = odd_keep.shape[1]

    def columns(quarter, count=1, size=width):
        return pl.ds(pl.multiple_of(quarter * size, 128), count * size)

    for c, keep, got in ((0, even_keep, even_got), (1, odd_keep, odd_got)):

        @pl.when(core == c)
        def _(keep=keep, got=got):
            out[:, columns(2 * core + y)] = keep[...]
            out[:, columns(2 * core + 1 - y)] = got[...]

    out[:, columns(2 * (1 - core), 2)] = crossed[...]
    kv_width = parts[0].shape[1] // 2
    for quarter, part in zip(quarters(), parts):
        k_out[:, columns(quarter, 1, kv_width)] = part[:, :kv_width].astype(BF16)
        v_out[:, columns(quarter, 1, kv_width)] = part[:, kv_width:].astype(BF16)


def body(queries, keys, values, grad_out, doc_ids):
    tok = queries.shape[0]
    n_blk, n_swap = lax.axis_size("blk"), lax.axis_size("swap")
    n_out = n_swap // 2
    seq_blk = tok * n_swap
    pair = 2 * tok
    far = -(-MOST // pair)
    q_width, kv_width = queries.shape[1] // 4, keys.shape[1] // 4
    both = ("swap", "blk")
    devices = [(b, s) for b in range(n_blk) for s in range(n_swap)]

    def index(b, s):
        return s * n_blk + b

    routes = [
        [(index(b, s), index(b ^ 1, s)) for b, s in devices],
        [(index(b, s), index(b, s ^ 1)) for b, s in devices],
        [(index(b, s), index(b ^ 1, s ^ 1)) for b, s in devices],
    ]

    def to_partners(parts):
        return [lax.ppermute(part, both, route) for part, route in zip(parts, routes)]

    def odd_route(k):
        return [(index(b, s), index(b, 2 * ((s // 2 + k) % n_out) + s % 2)) for b, s in devices]

    def even_route(k):
        route = []
        for b, s in devices:
            step, z = divmod(s // 2 + k, n_out)
            if b + 2 * step < n_blk:
                route.append((index(b, s), index(b + 2 * step, 2 * z + s % 2)))
        return route

    def along_z(parts, route_of, back=False):
        got = []
        for k, part in zip(shifts, parts):
            route = route_of(k)
            got.append(lax.ppermute(part, both, [(b, a) for a, b in route] if back else route))
        return got

    def along_x(part, step):
        return lax.ppermute(
            part, "blk", [(b, b + step) for b in range(n_blk) if 0 <= b + step < n_blk]
        )

    def shape(rows, cols, dtype=BF16):
        return jax.ShapeDtypeStruct((rows, cols), dtype)

    def split(a, b, width, groups, name, after=()):
        return vmem_call(
            functools.partial(split_kernel, groups),
            [shape(tok, 8 * width // len(groups))] * len(groups),
            (a, b),
            scratch=[pltpu.SemaphoreType.DMA((8,))],
            hbm=(0, 1),
            after=after,
            name=name,
        )

    shifts = [k for k in range(1, far + 1) if k < n_out]
    whole_ring = far == n_out
    block_shape = shape(pair, 2 * kv_width)
    sum_shape = shape(pair, 2 * kv_width, F32)

    one_each = [lambda numbers, i=i: [numbers[i]] for i in range(4)]
    by_core = [lambda numbers: [numbers[0] // 2 * 2 + i for i in (0, 1)], lambda numbers: [numbers[1] // 2 * 2 + i for i in (0, 1)]]
    kv_parts = split(keys, values, kv_width, one_each, "split_kv")
    kv_recv = to_partners(kv_parts[1:])
    mine, other = split(queries, grad_out, q_width, by_core, "split_qg")
    *made, other = vmem_call(
        functools.partial(payload_kernel, n_out, len(shifts)),
        [block_shape] * (2 + 2 * len(shifts)),
        (kv_parts[0], *kv_recv),
        through=(other,),
        name="payload",
    )
    crossed = lax.ppermute(other, both, routes[0])
    odd_qg, odd_send, even_qg, even_send = vmem_call(
        choose_kernel, [shape(tok, 2 * q_width)] * 4, (mine, crossed), after=(made[0],), name="choose_qg"
    )
    even, odd, *pays = made
    odd_got = along_z(pays[: len(shifts)], odd_route)
    odd_qg = (odd_qg, lax.ppermute(odd_send, both, routes[1]))
    even_got = along_z(pays[len(shifts) :], even_route)
    even_qg = (even_qg, lax.ppermute(even_send, both, routes[1]))
    rim = along_x(odd, 2) if whole_ring else None

    starts = doc_ids.reshape(-1, 128)
    n_slots = far + 1
    rows = 2 * (q_width // HEAD_DIM) * tok
    sum_shapes = [
        sum_shape if i == far or (i == 0 and whole_ring and which) else block_shape
        for which in (0, 1)
        for i in range(n_slots)
    ]

    def attend(which, slots, qg, after=()):
        return vmem_call(
            functools.partial(attend_kernel, which, n_slots, seq_blk),
            [shape(tok, q_width)] * 2 + sum_shapes[which * n_slots : (which + 1) * n_slots],
            (*qg, starts, doc_ids, *slots),
            scratch=[
                pltpu.VMEM((rows, 2 * HEAD_DIM), BF16),
                pltpu.VMEM((rows, HEAD_DIM), BF16),
                pltpu.VMEM((2, n_slots * pair, 2 * HEAD_DIM), BF16),
                pltpu.VMEM((n_slots * pair, HEAD_DIM), BF16),
                pltpu.VMEM((n_slots * pair, rows), F32),
                pltpu.VMEM((n_slots * pair, rows), F32),
                pltpu.VMEM((HEAD_DIM, rows), F32),
                pltpu.VMEM((n_slots * pair, 2 * HEAD_DIM), F32),
                pltpu.VMEM((3, 8, rows), F32),
                pltpu.VMEM((2, tok, q_width), BF16),
            ],
            smem=(3,),
            after=after,
            mib=32,
            flops=6_000_000_000,
            name="attend_odd" if which else "attend_even",
        )

    def slots_of(up, down, got):
        return [down if k == n_out else got[k - 1] for k in range(far, 0, -1)] + [up]

    def sent(sums):
        return [sums[far - k] for k in shifts]

    dq_odd, dq_odd_send, *odd_sums = attend(1, slots_of(odd, even, odd_got), odd_qg)
    odd_back = along_z(sent(odd_sums), odd_route, back=True)
    dq_even, dq_send, *even_sums = attend(0, slots_of(even, rim, even_got), even_qg, (dq_odd,))
    dq_odd_got = lax.ppermute(dq_odd_send, both, routes[1])
    odd_total, even_total, dq_send, *even_sent = vmem_call(
        functools.partial(odd_sum_kernel, n_out, len(shifts)),
        [sum_shape, sum_shape],
        (odd_sums[far], *odd_back, *([odd_sums[0]] if whole_ring else [])),
        after=(dq_odd_got,),
        through=[dq_send, *sent(even_sums)],
        name="odd_sum",
    )
    dq_even_got = lax.ppermute(dq_send, both, routes[1])
    even_back = along_z(even_sent, even_route, back=True)
    rim_home = (along_x(even_sums[0], -2),) if whole_ring else ()
    home = vmem_call(
        functools.partial(home_kernel, n_out, len(shifts)),
        [shape(tok, 2 * kv_width, F32)] + [shape(tok, 2 * kv_width)] * 3,
        (even_sums[far], odd_total, even_total, *even_back, *rim_home),
        scratch=[pltpu.VMEM((2, pair, 2 * kv_width), F32)],
        name="home",
    )
    kv_home = to_partners(home[1:])
    dq_parts = (dq_odd, dq_odd_got, dq_even, dq_even_got)
    (dq_cross,) = vmem_call(cross_kernel, [shape(tok, 2 * q_width)], dq_parts, after=(home[0],), name="cross")
    return vmem_call(
        finish_kernel,
        [shape(*queries.shape), shape(*keys.shape), shape(*values.shape)],
        (*dq_parts, lax.ppermute(dq_cross, both, routes[0]), home[0], *kv_home),
        name="finish",
    )


def solution(mesh):
    spec = P(("blk", "swap"), None)
    return jax.shard_map(
        lambda *args: tuple(body(*args)),
        mesh=mesh,
        in_specs=(spec, spec, spec, spec, P()),
        out_specs=(spec, spec, spec),
        check_vma=False,
    )
```

```python
import functools
import math

import jax
import jax.numpy as jnp
from jax import lax
from jax.experimental import pallas as pl
from jax.experimental.pallas import tpu as pltpu
from jax.sharding import PartitionSpec as P

HEAD_DIM = 128
MOST = 1024
BF16 = jnp.bfloat16
F32 = jnp.float32
LOG2E = 1.4426950408889634
MIB = 1024 * 1024

NN = (((1,), (0,)), ((), ()))
NT = (((1,), (1,)), ((), ()))
TN = (((0,), (0,)), ((), ()))


def dot(a, b, dims):
    return lax.dot_general(a, b, dims, preferred_element_type=F32)


def vmem_call(kernel, out_shapes, args, scratch=(), hbm=(), smem=(), after=(), through=(), mib=4, flops=0, name=None):
    def space(i):
        return pltpu.SMEM if i in smem else pltpu.HBM if i in hbm else pltpu.VMEM

    specs = [pl.BlockSpec(memory_space=space(i)) for i in range(len(args))]
    specs += [pl.BlockSpec(memory_space=pl.ANY)] * (len(after) + len(through))
    outs = [pl.BlockSpec(memory_space=pltpu.VMEM)] * len(out_shapes)
    outs += [pl.BlockSpec(memory_space=pl.ANY)] * len(through)
    n_args, n_out = len(args), len(out_shapes)
    n_in, n_made = len(specs), len(outs)

    def run(*refs):
        kernel(*refs[:n_args], *refs[n_in : n_in + n_out], *refs[n_in + n_made :])

    return pl.pallas_call(
        run,
        out_shape=list(out_shapes) + [jax.ShapeDtypeStruct(t.shape, t.dtype) for t in through],
        in_specs=specs,
        out_specs=outs,
        input_output_aliases={n_args + len(after) + i: n_out + i for i in range(len(through))},
        scratch_shapes=list(scratch),
        compiler_params=pltpu.CompilerParams(vmem_limit_bytes=mib * MIB),
        cost_estimate=pl.CostEstimate(flops=flops, bytes_accessed=0, transcendentals=0),
        name=name,
    )(*args, *after, *through)


def place():
    blk, swap = lax.axis_index("blk"), lax.axis_index("swap")
    return lax.rem(blk, 2), lax.rem(swap, 2), lax.div(swap, 2)


def quarters():
    core, y, _ = place()
    return [2 * core + y, 2 * (1 - core) + y, 2 * core + 1 - y, 2 * (1 - core) + 1 - y]


def split_kernel(groups, a_ref, b_ref, *rest):
    outs, sems = rest[:-1], rest[-1]
    width = a_ref.shape[1] // 4
    numbers = quarters()
    copies = []
    for group, out in zip(groups, outs):
        for i, member in enumerate(group(numbers)):
            columns = pl.ds(pl.multiple_of(member * width, 128), width)
            for j, src in enumerate((a_ref, b_ref)):
                dst = out.at[:, (2 * i + j) * width : (2 * i + j + 1) * width]
                copies.append(pltpu.make_async_copy(src.at[:, columns], dst, sems.at[len(copies)]))
    for copy in copies:
        copy.start()
    for copy in copies:
        copy.wait()


def choose_kernel(mine, got, *outs):
    core, y, _ = place()
    width = mine.shape[1] // 2
    for odd, (keep, send) in zip((1, 0), (outs[:2], outs[2:])):
        for out, yy in ((keep, y), (send, 1 - y)):
            columns = pl.ds(pl.multiple_of(yy * width, 128), width)

            @pl.when(core == odd)
            def _(out=out, columns=columns):
                out[...] = mine[:, columns]

            @pl.when(core != odd)
            def _(out=out, columns=columns):
                out[...] = got[:, columns]


def select_chunks(blocks, own, by_core, by_y, by_diag):
    core, y, _ = place()
    rows = own.shape[0]
    here = pl.ds(pl.multiple_of(y * rows, rows), rows)
    there = pl.ds(pl.multiple_of((1 - y) * rows, rows), rows)
    for c in (0, 1):

        @pl.when(core == c)
        def _(c=c):
            blocks[c][here, :] = own[...]
            blocks[c][there, :] = by_y[...]
            blocks[1 - c][here, :] = by_core[...]
            blocks[1 - c][there, :] = by_diag[...]


def fill_payloads(n_out, up, down, outs):
    _, _, z = place()
    for k, out in enumerate(outs, 1):

        @pl.when(z + k < n_out)
        def _(out=out):
            out[...] = up[...]

        @pl.when(z + k >= n_out)
        def _(out=out):
            out[...] = down[...]


def payload_kernel(n_out, own, by_core, by_y, by_diag, even, odd, pieces, *outs):
    select_chunks((even, odd), own, by_core, by_y, by_diag)
    _, _, z = place()
    rows = even.shape[0]
    for other in range(n_out):
        where = slice(other * rows, (other + 1) * rows)

        @pl.when(other > z)
        def _(where=where):
            pieces[where, :] = odd[...]

        @pl.when(other <= z)
        def _(where=where):
            pieces[where, :] = even[...]

    fill_payloads(n_out, even, odd, outs)


def attend_kernel(odd, n_out, n_slots, seq_blk, n_given, keep, by_y, starts, doc_scalars, *rest):
    given, rest = rest[:n_given], rest[n_given:]
    if not odd:
        dq_other, rest = rest[0], rest[1:]
    dq_keep, dq_send, rest = rest[0], rest[1], rest[2:]
    sums, rest = rest[:n_slots], rest[n_slots:]
    q_rows, g_rows, keys, vals, scores, dweights, dq_cols, acc, stats, dq_both = rest
    _, y, z = place()
    tok = keep.shape[0]
    width = keep.shape[1] // 2
    heads = width // HEAD_DIM
    pair = 2 * tok
    window = (n_slots - 1) * pair
    inv_root = 1.0 / math.sqrt(HEAD_DIM)
    scale = inv_root * LOG2E
    block = 2 * lax.div(lax.axis_index("blk"), 2) + odd
    first = block * seq_blk + z * pair
    base = first - window
    step_cols = 2 * tok
    n_steps = 2 * width // step_cols

    def stack(unit, src):
        for h in range(heads):
            rows = pl.ds(pl.multiple_of(unit * width + h * tok, tok), tok)
            q_rows[rows, :HEAD_DIM] = src[:, h * HEAD_DIM : (h + 1) * HEAD_DIM]
            g_rows[rows, :] = src[:, width + h * HEAD_DIM : width + (h + 1) * HEAD_DIM]

    stack(y, keep)
    stack(1 - y, by_y)
    unity = (
        lax.broadcasted_iota(jnp.int32, (tok, tok), 0) == lax.broadcasted_iota(jnp.int32, (tok, tok), 1)
    )
    unity = jnp.where(unity, 1.0, 0.0).astype(BF16)
    for h in range(2 * heads):
        rows = slice(h * tok, (h + 1) * tok)
        q_rows[rows, HEAD_DIM:] = unity
    for i in range(n_slots):
        rows = slice(i * pair, (i + 1) * pair)
        back = n_slots - 1 - i
        if n_given == n_slots:
            slot = given[i][...]
        elif back == 0:
            slot = given[2][...]
        elif back == n_out:
            slot = given[1][...]
        else:
            source = lax.rem(z + n_out - back, n_out)
            slot = given[0][pl.ds(pl.multiple_of(source * pair, pair), pair), :]
        for unit in (0, 1):
            keys[unit, rows, :HEAD_DIM] = slot[:, :HEAD_DIM]
        vals[rows, :] = slot[:, HEAD_DIM:]

    begin = lax.div(doc_scalars[first] - base, pair)
    begin_last = lax.div(doc_scalars[first + tok] - base, pair)

    def rows_of(j):
        return pl.ds(pl.multiple_of(j * pair, pair), pair)

    def cols_of(n):
        return slice(n * step_cols, (n + 1) * step_cols)

    def unit_of(n):
        return n * step_cols // width

    def fold(op, x):
        return op(x.reshape(x.shape[0] // 8, 8, x.shape[1]), axis=0)

    stats[0] = jnp.full(stats.shape[1:], -3e38, F32)
    stats[1] = jnp.zeros(stats.shape[1:], F32)
    stats[2] = jnp.zeros(stats.shape[1:], F32)
    dq_cols[...] = jnp.zeros_like(dq_cols)
    t = lax.broadcasted_iota(jnp.int32, (1, tok), 1)
    key_place = lax.broadcasted_iota(jnp.int32, (pair, tok), 0)
    lows = [starts[pl.ds(lax.div(first, 128) + unit, 1), :] for unit in (0, 1)]

    def columns_of(units):
        return [n for n in range(n_steps) if unit_of(n) in units]

    def over_slots(step):
        lax.fori_loop(begin, begin_last, functools.partial(step, (0,)), 0)
        lax.fori_loop(begin_last, n_slots, functools.partial(step, (0, 1)), 0)

    def score_step(units, j, carry):
        place_j = key_place + (base + j * pair)
        for unit in units:
            allowed = (place_j >= lows[unit]) & (place_j <= t + (first + unit * tok))
            keys[unit, rows_of(j), HEAD_DIM:] = jnp.where(allowed, 0.0, -1e30).astype(BF16)
        for n in columns_of(units):
            s = dot(keys[unit_of(n), rows_of(j), :], q_rows[cols_of(n), :], NT)
            scores[rows_of(j), cols_of(n)] = s
            stats[0, :, cols_of(n)] = jnp.maximum(stats[0, :, cols_of(n)], fold(jnp.max, s))
        return carry

    over_slots(score_step)
    for n in range(n_steps):
        top = jnp.max(stats[0, :, cols_of(n)], axis=0, keepdims=True)
        stats[0, :, cols_of(n)] = jnp.broadcast_to(top, (8, step_cols))

    def weight_step(units, j, carry):
        for n in columns_of(units):
            p = jnp.exp2((scores[rows_of(j), cols_of(n)] - stats[0, 0:1, cols_of(n)]) * scale)
            scores[rows_of(j), cols_of(n)] = p
            stats[1, :, cols_of(n)] += fold(jnp.sum, p)
            dweights[rows_of(j), cols_of(n)] = dot(vals[rows_of(j), :], g_rows[cols_of(n), :], NT)
        return carry

    over_slots(weight_step)
    for n in range(n_steps):
        inv = 1.0 / jnp.sum(stats[1, :, cols_of(n)], axis=0, keepdims=True)
        stats[1, :, cols_of(n)] = jnp.broadcast_to(inv, (8, step_cols))

    def value_step(units, j, carry):
        total = jnp.zeros((pair, HEAD_DIM), F32)
        for n in columns_of(units):
            d = dweights[rows_of(j), cols_of(n)]
            w = scores[rows_of(j), cols_of(n)] * stats[1, 0:1, cols_of(n)]
            wb = w.astype(BF16)
            total = total + dot(wb, g_rows[cols_of(n), :], NN)
            scores[rows_of(j), cols_of(n)] = w
            stats[2, :, cols_of(n)] += fold(jnp.sum, wb.astype(F32) * d)
        acc[rows_of(j), HEAD_DIM:] = total
        return carry

    over_slots(value_step)
    for n in range(n_steps):
        rowdot = jnp.sum(stats[2, :, cols_of(n)], axis=0, keepdims=True)
        stats[2, :, cols_of(n)] = jnp.broadcast_to(rowdot, (8, step_cols))

    def grad_step(units, j, carry):
        total = jnp.zeros((pair, HEAD_DIM), F32)
        k_cols = keys[0, rows_of(j), :HEAD_DIM].T
        for n in columns_of(units):
            rest = dweights[rows_of(j), cols_of(n)] - stats[2, 0:1, cols_of(n)]
            ds = (scores[rows_of(j), cols_of(n)] * rest).astype(BF16)
            total = total + dot(ds, q_rows[cols_of(n), :HEAD_DIM], NN)
            dq_cols[:, cols_of(n)] += dot(k_cols, ds, NN)
        acc[rows_of(j), :HEAD_DIM] = total * inv_root
        return carry

    over_slots(grad_step)

    for h in range(2 * heads):
        unit, head = h // heads, h % heads
        dq = (dq_cols[:, h * tok : (h + 1) * tok] * inv_root).T
        dq_both[unit, :, head * HEAD_DIM : (head + 1) * HEAD_DIM] = dq.astype(BF16)
    dq_keep[...] = dq_both[y]
    dq_send[:tok, :] = dq_both[1 - y]
    if not odd:
        dq_send[tok:, :] = dq_other[...]

    for i, out in enumerate(sums):

        @pl.when(i >= begin)
        def _(i=i, out=out):
            out[...] = acc[i * pair : (i + 1) * pair, :].astype(out.dtype)

        @pl.when(i < begin)
        def _(out=out):
            out[...] = jnp.zeros_like(out)


def add_terms(n_out, up, down, terms):
    _, _, z = place()
    for k, term in enumerate(terms, 1):
        value = term[...].astype(F32)
        wrapped = (z + k >= n_out).astype(F32)
        up = up + value * (1.0 - wrapped)
        down = down + value * wrapped
    return up, down


def odd_sum_kernel(n_out, n_terms, own_odd, *refs):
    terms, own_even, (odd_out, even_out) = refs[:n_terms], refs[n_terms:-2], refs[-2:]
    even = own_even[0][...] if own_even else jnp.zeros(even_out.shape, F32)
    odd_out[...], even_out[...] = add_terms(n_out, own_odd[...], even, terms)


def home_kernel(n_out, n_terms, own_even, odd_total, even_total, *refs):
    outs, total = refs[-5:-1], refs[-1]
    rim, terms = refs[: -5 - n_terms], refs[-5 - n_terms : -5]
    tok = own_even.shape[0] // 2
    odd = odd_total[...]
    if rim:
        odd = odd + rim[0][...].astype(F32)
    total[0], total[1] = add_terms(n_out, own_even[...] + even_total[...], odd, terms)
    core, y, _ = place()
    for out, c, yy in zip(outs, (core, 1 - core, core, 1 - core), (y, y, 1 - y, 1 - y)):
        out[...] = total[c, pl.ds(pl.multiple_of(yy * tok, tok), tok), :].astype(out.dtype)


def cross_kernel(odd_keep, even_keep, got_ref, out):
    core, y, _ = place()
    tok, width = odd_keep.shape
    even_got, odd_got = got_ref.at[:tok, :], got_ref.at[tok:, :]
    for c, keep, got in ((0, odd_keep, odd_got), (1, even_keep, even_got)):

        @pl.when(core == c)
        def _(keep=keep, got=got):
            out[:, pl.ds(pl.multiple_of(y * width, 128), width)] = keep[...]
            out[:, pl.ds(pl.multiple_of((1 - y) * width, 128), width)] = got[...]


def finish_kernel(odd_keep, even_keep, got_ref, crossed, *refs):
    parts, (out, k_out, v_out) = refs[:4], refs[4:]
    core, y, _ = place()
    tok, width = odd_keep.shape
    even_got, odd_got = got_ref.at[:tok, :], got_ref.at[tok:, :]

    def columns(quarter, count=1, size=width):
        return pl.ds(pl.multiple_of(quarter * size, 128), count * size)

    for c, keep, got in ((0, even_keep, even_got), (1, odd_keep, odd_got)):

        @pl.when(core == c)
        def _(keep=keep, got=got):
            out[:, columns(2 * core + y)] = keep[...]
            out[:, columns(2 * core + 1 - y)] = got[...]

    out[:, columns(2 * (1 - core), 2)] = crossed[...]
    kv_width = parts[0].shape[1] // 2
    for quarter, part in zip(quarters(), parts):
        k_out[:, columns(quarter, 1, kv_width)] = part[:, :kv_width].astype(BF16)
        v_out[:, columns(quarter, 1, kv_width)] = part[:, kv_width:].astype(BF16)


def body(queries, keys, values, grad_out, doc_ids):
    tok = queries.shape[0]
    n_blk, n_swap = lax.axis_size("blk"), lax.axis_size("swap")
    n_out = n_swap // 2
    seq_blk = tok * n_swap
    pair = 2 * tok
    far = -(-MOST // pair)
    q_width, kv_width = queries.shape[1] // 4, keys.shape[1] // 4
    both = ("swap", "blk")
    devices = [(b, s) for b in range(n_blk) for s in range(n_swap)]

    def index(b, s):
        return s * n_blk + b

    routes = [
        [(index(b, s), index(b ^ 1, s)) for b, s in devices],
        [(index(b, s), index(b, s ^ 1)) for b, s in devices],
        [(index(b, s), index(b ^ 1, s ^ 1)) for b, s in devices],
    ]

    def to_partners(parts):
        return [lax.ppermute(part, both, route) for part, route in zip(parts, routes)]

    def odd_route(k):
        return [(index(b, s), index(b, 2 * ((s // 2 + k) % n_out) + s % 2)) for b, s in devices]

    def even_route(k):
        route = []
        for b, s in devices:
            step, z = divmod(s // 2 + k, n_out)
            if b + 2 * step < n_blk:
                route.append((index(b, s), index(b + 2 * step, 2 * z + s % 2)))
        return route

    def along_z(parts, route_of, back=False):
        got = []
        for k, part in zip(shifts, parts):
            route = route_of(k)
            got.append(lax.ppermute(part, both, [(b, a) for a, b in route] if back else route))
        return got

    def gathered(pieces):
        groups = [[2 * z + y for z in range(n_out)] for y in (0, 1)]
        got = lax.all_to_all(
            pieces.reshape(n_out, pair, -1), "swap", 0, 0, axis_index_groups=groups
        )
        return got.reshape(pieces.shape)

    def along_x(part, step):
        return lax.ppermute(
            part, "blk", [(b, b + step) for b in range(n_blk) if 0 <= b + step < n_blk]
        )

    def shape(rows, cols, dtype=BF16):
        return jax.ShapeDtypeStruct((rows, cols), dtype)

    def split(a, b, width, groups, name, after=()):
        return vmem_call(
            functools.partial(split_kernel, groups),
            [shape(tok, 8 * width // len(groups))] * len(groups),
            (a, b),
            scratch=[pltpu.SemaphoreType.DMA((8,))],
            hbm=(0, 1),
            after=after,
            name=name,
        )

    shifts = [k for k in range(1, far + 1) if k < n_out]
    whole_ring = far == n_out
    block_shape = shape(pair, 2 * kv_width)
    sum_shape = shape(pair, 2 * kv_width, F32)

    one_each = [lambda numbers, i=i: [numbers[i]] for i in range(4)]
    by_core = [lambda numbers: [numbers[0] // 2 * 2 + i for i in (0, 1)], lambda numbers: [numbers[1] // 2 * 2 + i for i in (0, 1)]]
    kv_parts = [
        jnp.concatenate(
            [lax.dynamic_slice_in_dim(x, quarter * kv_width, kv_width, 1) for x in (keys, values)], 1
        )
        for quarter in quarters()
    ]
    kv_recv = to_partners(kv_parts[1:])
    half = 2 * q_width

    def halves(which):
        parts = [lax.dynamic_slice_in_dim(x, which * half, half, 1) for x in (queries, grad_out)]
        return jnp.concatenate(
            [x[:, i * q_width : (i + 1) * q_width] for i in (0, 1) for x in parts], 1
        )

    core = place()[0]
    mine, other = halves(core), halves(1 - core)
    *made, other = vmem_call(
        functools.partial(payload_kernel, n_out),
        [block_shape] * 2 + [shape(n_out * pair, 2 * kv_width)] + [block_shape] * len(shifts),
        (kv_parts[0], *kv_recv),
        through=(other,),
        name="payload",
    )
    crossed = lax.ppermute(other, both, routes[0])
    odd_qg, odd_send, even_qg, even_send = vmem_call(
        choose_kernel, [shape(tok, 2 * q_width)] * 4, (mine, crossed), after=(made[0],), name="choose_qg"
    )
    even, odd, odd_pieces, *pays = made
    odd_got = gathered(odd_pieces)
    odd_qg = (odd_qg, lax.ppermute(odd_send, both, routes[1]))
    even_got = along_z(pays, even_route)
    even_qg = (even_qg, lax.ppermute(even_send, both, routes[1]))
    rim = along_x(odd, 2) if whole_ring else None

    starts = doc_ids.reshape(-1, 128)
    n_slots = far + 1
    rows = 2 * (q_width // HEAD_DIM) * tok
    sum_shapes = [
        sum_shape if i == far or (i == 0 and whole_ring and which) else block_shape
        for which in (0, 1)
        for i in range(n_slots)
    ]

    def attend(which, slots, qg, dq_other=None):
        return vmem_call(
            functools.partial(attend_kernel, which, n_out, n_slots, seq_blk, len(slots)),
            [shape(tok, q_width), shape(tok if which else pair, q_width)]
            + sum_shapes[which * n_slots : (which + 1) * n_slots],
            (*qg, starts, doc_ids, *slots) + (() if which else (dq_other,)),
            scratch=[
                pltpu.VMEM((rows, 2 * HEAD_DIM), BF16),
                pltpu.VMEM((rows, HEAD_DIM), BF16),
                pltpu.VMEM((2, n_slots * pair, 2 * HEAD_DIM), BF16),
                pltpu.VMEM((n_slots * pair, HEAD_DIM), BF16),
                pltpu.VMEM((n_slots * pair, rows), F32),
                pltpu.VMEM((n_slots * pair, rows), F32),
                pltpu.VMEM((HEAD_DIM, rows), F32),
                pltpu.VMEM((n_slots * pair, 2 * HEAD_DIM), F32),
                pltpu.VMEM((3, 8, rows), F32),
                pltpu.VMEM((2, tok, q_width), BF16),
            ],
            smem=(3,),
            mib=28,
            flops=6_000_000_000,
            name="attend_odd" if which else "attend_even",
        )

    def slots_of(up, down, got):
        return [down if k == n_out else got[k - 1] for k in range(far, 0, -1)] + [up]

    def sent(sums):
        return [sums[far - k] for k in shifts]

    dq_odd, dq_odd_send, *odd_sums = attend(1, (odd_got, even, odd), odd_qg)
    odd_back = along_z(sent(odd_sums), odd_route, back=True)
    dq_even, dq_send, *even_sums = attend(0, slots_of(even, rim, even_got), even_qg, dq_odd_send)
    odd_total, even_total, dq_send, *even_sent = vmem_call(
        functools.partial(odd_sum_kernel, n_out, len(shifts)),
        [sum_shape, sum_shape],
        (odd_sums[far], *odd_back, *([odd_sums[0]] if whole_ring else [])),
        through=[dq_send, *sent(even_sums)],
        name="odd_sum",
    )
    dq_got = lax.ppermute(dq_send, both, routes[1])
    rim_home = (along_x(even_sums[0], -2),) if whole_ring else ()
    even_back = along_z(even_sent, even_route, back=True)
    home = vmem_call(
        functools.partial(home_kernel, n_out, len(shifts)),
        [shape(tok, 2 * kv_width, F32)] + [shape(tok, 2 * kv_width)] * 3,
        (even_sums[far], odd_total, even_total, *rim_home, *even_back),
        scratch=[pltpu.VMEM((2, pair, 2 * kv_width), F32)],
        name="home",
    )
    kv_home = to_partners(home[1:])
    dq_parts = (dq_odd, dq_even, dq_got)
    (dq_cross,) = vmem_call(cross_kernel, [shape(tok, 2 * q_width)], dq_parts, after=(home[0],), name="cross")
    return vmem_call(
        finish_kernel,
        [shape(*queries.shape), shape(*keys.shape), shape(*values.shape)],
        (*dq_parts, lax.ppermute(dq_cross, both, routes[0]), home[0], *kv_home),
        name="finish",
    )


def solution(mesh):
    spec = P(("blk", "swap"), None)
    return jax.shard_map(
        lambda *args: tuple(body(*args)),
        mesh=mesh,
        in_specs=(spec, spec, spec, spec, P()),
        out_specs=(spec, spec, spec),
        check_vma=False,
    )
```

```python
import functools
import math

import jax
import jax.numpy as jnp
from jax import lax
from jax.experimental import pallas as pl
from jax.experimental.pallas import tpu as pltpu
from jax.sharding import PartitionSpec as P

HEAD_DIM = 128
MOST = 1024
BF16 = jnp.bfloat16
F32 = jnp.float32
LOG2E = 1.4426950408889634
MIB = 1024 * 1024

NN = (((1,), (0,)), ((), ()))
NT = (((1,), (1,)), ((), ()))
TN = (((0,), (0,)), ((), ()))


def dot(a, b, dims):
    return lax.dot_general(a, b, dims, preferred_element_type=F32)


def vmem_call(kernel, out_shapes, args, scratch=(), hbm=(), smem=(), after=(), through=(), mib=4, flops=0, name=None):
    def space(i):
        return pltpu.SMEM if i in smem else pltpu.HBM if i in hbm else pltpu.VMEM

    specs = [pl.BlockSpec(memory_space=space(i)) for i in range(len(args))]
    specs += [pl.BlockSpec(memory_space=pl.ANY)] * (len(after) + len(through))
    outs = [pl.BlockSpec(memory_space=pltpu.VMEM)] * len(out_shapes)
    outs += [pl.BlockSpec(memory_space=pl.ANY)] * len(through)
    n_args, n_out = len(args), len(out_shapes)
    n_in, n_made = len(specs), len(outs)

    def run(*refs):
        kernel(*refs[:n_args], *refs[n_in : n_in + n_out], *refs[n_in + n_made :])

    return pl.pallas_call(
        run,
        out_shape=list(out_shapes) + [jax.ShapeDtypeStruct(t.shape, t.dtype) for t in through],
        in_specs=specs,
        out_specs=outs,
        input_output_aliases={n_args + len(after) + i: n_out + i for i in range(len(through))},
        scratch_shapes=list(scratch),
        compiler_params=pltpu.CompilerParams(vmem_limit_bytes=mib * MIB),
        cost_estimate=pl.CostEstimate(flops=flops, bytes_accessed=0, transcendentals=0),
        name=name,
    )(*args, *after, *through)


def place():
    blk, swap = lax.axis_index("blk"), lax.axis_index("swap")
    return lax.rem(blk, 2), lax.rem(swap, 2), lax.div(swap, 2)


def quarters():
    core, y, _ = place()
    return [2 * core + y, 2 * (1 - core) + y, 2 * core + 1 - y, 2 * (1 - core) + 1 - y]


def split_kernel(groups, a_ref, b_ref, *rest):
    outs, sems = rest[:-1], rest[-1]
    width = a_ref.shape[1] // 4
    numbers = quarters()
    copies = []
    for group, out in zip(groups, outs):
        for i, member in enumerate(group(numbers)):
            columns = pl.ds(pl.multiple_of(member * width, 128), width)
            for j, src in enumerate((a_ref, b_ref)):
                dst = out.at[:, (2 * i + j) * width : (2 * i + j + 1) * width]
                copies.append(pltpu.make_async_copy(src.at[:, columns], dst, sems.at[len(copies)]))
    for copy in copies:
        copy.start()
    for copy in copies:
        copy.wait()


def choose_kernel(mine, got, *outs):
    core, y, _ = place()
    width = mine.shape[1] // 2
    for odd, (keep, send) in zip((1, 0), (outs[:2], outs[2:])):
        for out, yy in ((keep, y), (send, 1 - y)):
            columns = pl.ds(pl.multiple_of(yy * width, 128), width)

            @pl.when(core == odd)
            def _(out=out, columns=columns):
                out[...] = mine[:, columns]

            @pl.when(core != odd)
            def _(out=out, columns=columns):
                out[...] = got[:, columns]


def select_chunks(blocks, own, by_core, by_y, by_diag):
    core, y, _ = place()
    rows = own.shape[0]
    here = pl.ds(pl.multiple_of(y * rows, rows), rows)
    there = pl.ds(pl.multiple_of((1 - y) * rows, rows), rows)
    for c in (0, 1):

        @pl.when(core == c)
        def _(c=c):
            blocks[c][here, :] = own[...]
            blocks[c][there, :] = by_y[...]
            blocks[1 - c][here, :] = by_core[...]
            blocks[1 - c][there, :] = by_diag[...]


def fill_payloads(n_out, up, down, outs):
    _, _, z = place()
    for k, out in enumerate(outs, 1):

        @pl.when(z + k < n_out)
        def _(out=out):
            out[...] = up[...]

        @pl.when(z + k >= n_out)
        def _(out=out):
            out[...] = down[...]


def payload_kernel(n_out, own, by_core, by_y, by_diag, even, odd, pieces, *outs):
    select_chunks((even, odd), own, by_core, by_y, by_diag)
    _, _, z = place()
    rows = even.shape[0]
    for other in range(n_out):
        where = slice(other * rows, (other + 1) * rows)

        @pl.when(other > z)
        def _(where=where):
            pieces[where, :] = odd[...]

        @pl.when(other <= z)
        def _(where=where):
            pieces[where, :] = even[...]

    fill_payloads(n_out, even, odd, outs)


def attend_kernel(odd, n_out, n_slots, seq_blk, n_given, keep, by_y, starts, doc_scalars, *rest):
    given, rest = rest[:n_given], rest[n_given:]
    if not odd:
        dq_other, rest = rest[0], rest[1:]
    dq_keep, dq_send, rest = rest[0], rest[1], rest[2:]
    sums, rest = rest[:n_slots], rest[n_slots:]
    q_rows, g_rows, keys, vals, scores, dweights, dq_cols, acc, stats, dq_both = rest
    _, y, z = place()
    tok = keep.shape[0]
    width = keep.shape[1] // 2
    heads = width // HEAD_DIM
    pair = 2 * tok
    window = (n_slots - 1) * pair
    inv_root = 1.0 / math.sqrt(HEAD_DIM)
    scale = inv_root * LOG2E
    block = 2 * lax.div(lax.axis_index("blk"), 2) + odd
    first = block * seq_blk + z * pair
    base = first - window
    step_cols = 2 * tok
    n_steps = 2 * width // step_cols

    def stack(unit, src):
        for h in range(heads):
            rows = pl.ds(pl.multiple_of(unit * width + h * tok, tok), tok)
            q_rows[rows, :HEAD_DIM] = src[:, h * HEAD_DIM : (h + 1) * HEAD_DIM]
            g_rows[rows, :] = src[:, width + h * HEAD_DIM : width + (h + 1) * HEAD_DIM]

    stack(y, keep)
    stack(1 - y, by_y)
    unity = (
        lax.broadcasted_iota(jnp.int32, (tok, tok), 0) == lax.broadcasted_iota(jnp.int32, (tok, tok), 1)
    )
    unity = jnp.where(unity, 1.0, 0.0).astype(BF16)
    for h in range(2 * heads):
        rows = slice(h * tok, (h + 1) * tok)
        q_rows[rows, HEAD_DIM:] = unity
    for i in range(n_slots):
        rows = slice(i * pair, (i + 1) * pair)
        back = n_slots - 1 - i
        if n_given == n_slots:
            slot = given[i][...]
        elif back == 0:
            slot = given[2][...]
        elif back == n_out:
            slot = given[1][...]
        else:
            source = lax.rem(z + n_out - back, n_out)
            slot = given[0][pl.ds(pl.multiple_of(source * pair, pair), pair), :]
        for unit in (0, 1):
            keys[unit, rows, :HEAD_DIM] = slot[:, :HEAD_DIM]
        vals[rows, :] = slot[:, HEAD_DIM:]

    begin = lax.div(doc_scalars[first] - base, pair)
    begin_last = lax.div(doc_scalars[first + tok] - base, pair)

    def rows_of(j):
        return pl.ds(pl.multiple_of(j * pair, pair), pair)

    def cols_of(n):
        return slice(n * step_cols, (n + 1) * step_cols)

    def unit_of(n):
        return n * step_cols // width

    def fold(op, x):
        return op(x.reshape(x.shape[0] // 8, 8, x.shape[1]), axis=0)

    stats[0] = jnp.full(stats.shape[1:], -3e38, F32)
    stats[1] = jnp.zeros(stats.shape[1:], F32)
    stats[2] = jnp.zeros(stats.shape[1:], F32)
    dq_cols[...] = jnp.zeros_like(dq_cols)
    t = lax.broadcasted_iota(jnp.int32, (1, tok), 1)
    key_place = lax.broadcasted_iota(jnp.int32, (pair, tok), 0)
    lows = [starts[pl.ds(lax.div(first, 128) + unit, 1), :] for unit in (0, 1)]

    def columns_of(units):
        return [n for n in range(n_steps) if unit_of(n) in units]

    def over_slots(step):
        lax.fori_loop(begin, begin_last, functools.partial(step, (0,)), 0)
        lax.fori_loop(begin_last, n_slots, functools.partial(step, (0, 1)), 0)

    def score_step(units, j, carry):
        place_j = key_place + (base + j * pair)
        for unit in units:
            allowed = (place_j >= lows[unit]) & (place_j <= t + (first + unit * tok))
            keys[unit, rows_of(j), HEAD_DIM:] = jnp.where(allowed, 0.0, -1e30).astype(BF16)
        for n in columns_of(units):
            s = dot(keys[unit_of(n), rows_of(j), :], q_rows[cols_of(n), :], NT)
            scores[rows_of(j), cols_of(n)] = s
            stats[0, :, cols_of(n)] = jnp.maximum(stats[0, :, cols_of(n)], fold(jnp.max, s))
        return carry

    over_slots(score_step)
    for n in range(n_steps):
        top = jnp.max(stats[0, :, cols_of(n)], axis=0, keepdims=True)
        stats[0, :, cols_of(n)] = jnp.broadcast_to(top, (8, step_cols))

    def weight_step(units, j, carry):
        for n in columns_of(units):
            p = jnp.exp2((scores[rows_of(j), cols_of(n)] - stats[0, 0:1, cols_of(n)]) * scale)
            scores[rows_of(j), cols_of(n)] = p
            stats[1, :, cols_of(n)] += fold(jnp.sum, p)
            dweights[rows_of(j), cols_of(n)] = dot(vals[rows_of(j), :], g_rows[cols_of(n), :], NT)
        return carry

    over_slots(weight_step)
    for n in range(n_steps):
        inv = 1.0 / jnp.sum(stats[1, :, cols_of(n)], axis=0, keepdims=True)
        stats[1, :, cols_of(n)] = jnp.broadcast_to(inv, (8, step_cols))

    def value_step(units, j, carry):
        total = jnp.zeros((pair, HEAD_DIM), F32)
        for n in columns_of(units):
            d = dweights[rows_of(j), cols_of(n)]
            w = scores[rows_of(j), cols_of(n)] * stats[1, 0:1, cols_of(n)]
            wb = w.astype(BF16)
            total = total + dot(wb, g_rows[cols_of(n), :], NN)
            scores[rows_of(j), cols_of(n)] = w
            stats[2, :, cols_of(n)] += fold(jnp.sum, wb.astype(F32) * d)
        acc[rows_of(j), HEAD_DIM:] = total
        return carry

    over_slots(value_step)
    for n in range(n_steps):
        rowdot = jnp.sum(stats[2, :, cols_of(n)], axis=0, keepdims=True)
        stats[2, :, cols_of(n)] = jnp.broadcast_to(rowdot, (8, step_cols))

    def grad_step(units, j, carry):
        total = jnp.zeros((pair, HEAD_DIM), F32)
        k_cols = keys[0, rows_of(j), :HEAD_DIM].T
        for n in columns_of(units):
            rest = dweights[rows_of(j), cols_of(n)] - stats[2, 0:1, cols_of(n)]
            ds = (scores[rows_of(j), cols_of(n)] * rest).astype(BF16)
            total = total + dot(ds, q_rows[cols_of(n), :HEAD_DIM], NN)
            dq_cols[:, cols_of(n)] += dot(k_cols, ds, NN)
        acc[rows_of(j), :HEAD_DIM] = total * inv_root
        return carry

    over_slots(grad_step)

    for h in range(2 * heads):
        unit, head = h // heads, h % heads
        dq = (dq_cols[:, h * tok : (h + 1) * tok] * inv_root).T
        dq_both[unit, :, head * HEAD_DIM : (head + 1) * HEAD_DIM] = dq.astype(BF16)
    dq_keep[...] = dq_both[y]
    dq_send[:tok, :] = dq_both[1 - y]
    if not odd:
        dq_send[tok:, :] = dq_other[...]

    for i, out in enumerate(sums):

        @pl.when(i >= begin)
        def _(i=i, out=out):
            out[...] = acc[i * pair : (i + 1) * pair, :].astype(out.dtype)

        @pl.when(i < begin)
        def _(out=out):
            out[...] = jnp.zeros_like(out)


def swapped(parts):
    return [*parts[1:2], *parts[:1], *parts[2:]]


def add_terms(n_out, up, down, terms):
    _, _, z = place()
    for k, term in enumerate(terms, 1):
        value = term[...].astype(F32)
        wrapped = (z + k >= n_out).astype(F32)
        up = up + value * (1.0 - wrapped)
        down = down + value * wrapped
    return up, down


def odd_sum_kernel(n_out, n_terms, own_odd, *refs):
    terms, own_even, (odd_out, even_out) = swapped(refs[:n_terms]), refs[n_terms:-2], refs[-2:]
    even = own_even[0][...] if own_even else jnp.zeros(even_out.shape, F32)
    odd_out[...], even_out[...] = add_terms(n_out, own_odd[...], even, terms)


def home_kernel(n_out, n_terms, own_even, odd_total, even_total, *refs):
    outs, total = refs[-5:-1], refs[-1]
    rim, terms = refs[: -5 - n_terms], refs[-5 - n_terms : -5]
    terms = swapped(terms)
    tok = own_even.shape[0] // 2
    odd = odd_total[...]
    if rim:
        odd = odd + rim[0][...].astype(F32)
    total[0], total[1] = add_terms(n_out, own_even[...] + even_total[...], odd, terms)
    core, y, _ = place()
    for out, c, yy in zip(outs, (core, 1 - core, core, 1 - core), (y, y, 1 - y, 1 - y)):
        out[...] = total[c, pl.ds(pl.multiple_of(yy * tok, tok), tok), :].astype(out.dtype)


def cross_kernel(odd_keep, even_keep, got_ref, out):
    core, y, _ = place()
    tok, width = odd_keep.shape
    even_got, odd_got = got_ref.at[:tok, :], got_ref.at[tok:, :]
    for c, keep, got in ((0, odd_keep, odd_got), (1, even_keep, even_got)):

        @pl.when(core == c)
        def _(keep=keep, got=got):
            out[:, pl.ds(pl.multiple_of(y * width, 128), width)] = keep[...]
            out[:, pl.ds(pl.multiple_of((1 - y) * width, 128), width)] = got[...]


def finish_kernel(odd_keep, even_keep, got_ref, crossed, *refs):
    parts, (out, k_out, v_out) = refs[:4], refs[4:]
    core, y, _ = place()
    tok, width = odd_keep.shape
    even_got, odd_got = got_ref.at[:tok, :], got_ref.at[tok:, :]

    def columns(quarter, count=1, size=width):
        return pl.ds(pl.multiple_of(quarter * size, 128), count * size)

    for c, keep, got in ((0, even_keep, even_got), (1, odd_keep, odd_got)):

        @pl.when(core == c)
        def _(keep=keep, got=got):
            out[:, columns(2 * core + y)] = keep[...]
            out[:, columns(2 * core + 1 - y)] = got[...]

    out[:, columns(2 * (1 - core), 2)] = crossed[...]
    kv_width = parts[0].shape[1] // 2
    for quarter, part in zip(quarters(), parts):
        k_out[:, columns(quarter, 1, kv_width)] = part[:, :kv_width].astype(BF16)
        v_out[:, columns(quarter, 1, kv_width)] = part[:, kv_width:].astype(BF16)


def body(queries, keys, values, grad_out, doc_ids):
    tok = queries.shape[0]
    n_blk, n_swap = lax.axis_size("blk"), lax.axis_size("swap")
    n_out = n_swap // 2
    seq_blk = tok * n_swap
    pair = 2 * tok
    far = -(-MOST // pair)
    q_width, kv_width = queries.shape[1] // 4, keys.shape[1] // 4
    both = ("swap", "blk")
    devices = [(b, s) for b in range(n_blk) for s in range(n_swap)]

    def index(b, s):
        return s * n_blk + b

    routes = [
        [(index(b, s), index(b ^ 1, s)) for b, s in devices],
        [(index(b, s), index(b, s ^ 1)) for b, s in devices],
        [(index(b, s), index(b ^ 1, s ^ 1)) for b, s in devices],
    ]

    def to_partners(parts):
        return [lax.ppermute(part, both, route) for part, route in zip(parts, routes)]

    def odd_route(k):
        return [(index(b, s), index(b, 2 * ((s // 2 + k) % n_out) + s % 2)) for b, s in devices]

    def even_route(k):
        route = []
        for b, s in devices:
            step, z = divmod(s // 2 + k, n_out)
            if b + 2 * step < n_blk:
                route.append((index(b, s), index(b + 2 * step, 2 * z + s % 2)))
        return route

    def along_z(parts, route_of, back=False):
        got = []
        for k, part in zip(shifts, parts):
            route = route_of(k)
            got.append(lax.ppermute(part, both, [(b, a) for a, b in route] if back else route))
        return got

    def gathered(pieces):
        groups = [[2 * z + y for z in range(n_out)] for y in (0, 1)]
        got = lax.all_to_all(
            pieces.reshape(n_out, pair, -1), "swap", 0, 0, axis_index_groups=groups
        )
        return got.reshape(pieces.shape)

    def along_x(part, step):
        return lax.ppermute(
            part, "blk", [(b, b + step) for b in range(n_blk) if 0 <= b + step < n_blk]
        )

    def shape(rows, cols, dtype=BF16):
        return jax.ShapeDtypeStruct((rows, cols), dtype)

    def split(a, b, width, groups, name, after=()):
        return vmem_call(
            functools.partial(split_kernel, groups),
            [shape(tok, 8 * width // len(groups))] * len(groups),
            (a, b),
            scratch=[pltpu.SemaphoreType.DMA((8,))],
            hbm=(0, 1),
            after=after,
            name=name,
        )

    shifts = [k for k in range(1, far + 1) if k < n_out]
    whole_ring = far == n_out
    block_shape = shape(pair, 2 * kv_width)
    sum_shape = shape(pair, 2 * kv_width, F32)

    one_each = [lambda numbers, i=i: [numbers[i]] for i in range(4)]
    by_core = [lambda numbers: [numbers[0] // 2 * 2 + i for i in (0, 1)], lambda numbers: [numbers[1] // 2 * 2 + i for i in (0, 1)]]
    kv_parts = [
        jnp.concatenate(
            [lax.dynamic_slice_in_dim(x, quarter * kv_width, kv_width, 1) for x in (keys, values)], 1
        )
        for quarter in quarters()
    ]
    kv_recv = to_partners(kv_parts[1:])
    half = 2 * q_width

    def halves(which):
        parts = [lax.dynamic_slice_in_dim(x, which * half, half, 1) for x in (queries, grad_out)]
        return jnp.concatenate(
            [x[:, i * q_width : (i + 1) * q_width] for i in (0, 1) for x in parts], 1
        )

    core = place()[0]
    mine, other = halves(core), halves(1 - core)
    *made, other = vmem_call(
        functools.partial(payload_kernel, n_out),
        [block_shape] * 2 + [shape(n_out * pair, 2 * kv_width)] + [block_shape] * len(shifts),
        (kv_parts[0], *kv_recv),
        through=(other,),
        name="payload",
    )
    crossed = lax.ppermute(other, both, routes[0])
    odd_qg, odd_send, even_qg, even_send = vmem_call(
        choose_kernel, [shape(tok, 2 * q_width)] * 4, (mine, crossed), after=(made[0],), name="choose_qg"
    )
    even, odd, odd_pieces, *pays = made
    odd_got = gathered(odd_pieces)
    odd_qg = (odd_qg, lax.ppermute(odd_send, both, routes[1]))
    even_got = along_z(pays, even_route)
    even_qg = (even_qg, lax.ppermute(even_send, both, routes[1]))
    rim = along_x(odd, 2) if whole_ring else None

    starts = doc_ids.reshape(-1, 128)
    n_slots = far + 1
    rows = 2 * (q_width // HEAD_DIM) * tok
    sum_shapes = [
        sum_shape if i == far or (i == 0 and whole_ring and which) else block_shape
        for which in (0, 1)
        for i in range(n_slots)
    ]

    def attend(which, slots, qg, dq_other=None):
        return vmem_call(
            functools.partial(attend_kernel, which, n_out, n_slots, seq_blk, len(slots)),
            [shape(tok, q_width), shape(tok if which else pair, q_width)]
            + sum_shapes[which * n_slots : (which + 1) * n_slots],
            (*qg, starts, doc_ids, *slots) + (() if which else (dq_other,)),
            scratch=[
                pltpu.VMEM((rows, 2 * HEAD_DIM), BF16),
                pltpu.VMEM((rows, HEAD_DIM), BF16),
                pltpu.VMEM((2, n_slots * pair, 2 * HEAD_DIM), BF16),
                pltpu.VMEM((n_slots * pair, HEAD_DIM), BF16),
                pltpu.VMEM((n_slots * pair, rows), F32),
                pltpu.VMEM((n_slots * pair, rows), F32),
                pltpu.VMEM((HEAD_DIM, rows), F32),
                pltpu.VMEM((n_slots * pair, 2 * HEAD_DIM), F32),
                pltpu.VMEM((3, 8, rows), F32),
                pltpu.VMEM((2, tok, q_width), BF16),
            ],
            smem=(3,),
            mib=28,
            flops=6_000_000_000,
            name="attend_odd" if which else "attend_even",
        )

    def slots_of(up, down, got):
        return [down if k == n_out else got[k - 1] for k in range(far, 0, -1)] + [up]

    def sent(sums):
        return [sums[far - k] for k in shifts]

    dq_odd, dq_odd_send, *odd_sums = attend(1, (odd_got, even, odd), odd_qg)
    odd_back = along_z(sent(odd_sums), odd_route, back=True)
    dq_even, dq_send, *even_sums = attend(0, slots_of(even, rim, even_got), even_qg, dq_odd_send)
    odd_total, even_total, dq_send, *even_sent = vmem_call(
        functools.partial(odd_sum_kernel, n_out, len(shifts)),
        [sum_shape, sum_shape],
        (odd_sums[far], *swapped(odd_back), *([odd_sums[0]] if whole_ring else [])),
        through=[dq_send, *sent(even_sums)],
        name="odd_sum",
    )
    dq_got = lax.ppermute(dq_send, both, routes[1])
    rim_home = (along_x(even_sums[0], -2),) if whole_ring else ()
    even_back = along_z(even_sent, even_route, back=True)
    home = vmem_call(
        functools.partial(home_kernel, n_out, len(shifts)),
        [shape(tok, 2 * kv_width, F32)] + [shape(tok, 2 * kv_width)] * 3,
        (even_sums[far], odd_total, even_total, *rim_home, *swapped(even_back)),
        scratch=[pltpu.VMEM((2, pair, 2 * kv_width), F32)],
        name="home",
    )
    kv_home = to_partners(home[1:])
    dq_parts = (dq_odd, dq_even, dq_got)
    (dq_cross,) = vmem_call(cross_kernel, [shape(tok, 2 * q_width)], dq_parts, after=(home[0],), name="cross")
    return vmem_call(
        finish_kernel,
        [shape(*queries.shape), shape(*keys.shape), shape(*values.shape)],
        (*dq_parts, lax.ppermute(dq_cross, both, routes[0]), home[0], *kv_home),
        name="finish",
    )


def solution(mesh):
    spec = P(("blk", "swap"), None)
    return jax.shard_map(
        lambda *args: tuple(body(*args)),
        mesh=mesh,
        in_specs=(spec, spec, spec, spec, P()),
        out_specs=(spec, spec, spec),
        check_vma=False,
    )
```

```python
import functools
import math

import jax
import jax.numpy as jnp
from jax import lax
from jax.experimental import pallas as pl
from jax.experimental.pallas import tpu as pltpu
from jax.sharding import PartitionSpec as P

HEAD_DIM = 128
MOST = 1024
BF16 = jnp.bfloat16
F32 = jnp.float32
LOG2E = 1.4426950408889634
MIB = 1024 * 1024

NN = (((1,), (0,)), ((), ()))
NT = (((1,), (1,)), ((), ()))
TN = (((0,), (0,)), ((), ()))


def dot(a, b, dims):
    return lax.dot_general(a, b, dims, preferred_element_type=F32)


def vmem_call(kernel, out_shapes, args, scratch=(), hbm=(), smem=(), after=(), through=(), mib=4, flops=0, name=None):
    def space(i):
        return pltpu.SMEM if i in smem else pltpu.HBM if i in hbm else pltpu.VMEM

    specs = [pl.BlockSpec(memory_space=space(i)) for i in range(len(args))]
    specs += [pl.BlockSpec(memory_space=pl.ANY)] * (len(after) + len(through))
    outs = [pl.BlockSpec(memory_space=pltpu.VMEM)] * len(out_shapes)
    outs += [pl.BlockSpec(memory_space=pl.ANY)] * len(through)
    n_args, n_out = len(args), len(out_shapes)
    n_in, n_made = len(specs), len(outs)

    def run(*refs):
        kernel(*refs[:n_args], *refs[n_in : n_in + n_out], *refs[n_in + n_made :])

    return pl.pallas_call(
        run,
        out_shape=list(out_shapes) + [jax.ShapeDtypeStruct(t.shape, t.dtype) for t in through],
        in_specs=specs,
        out_specs=outs,
        input_output_aliases={n_args + len(after) + i: n_out + i for i in range(len(through))},
        scratch_shapes=list(scratch),
        compiler_params=pltpu.CompilerParams(vmem_limit_bytes=mib * MIB),
        cost_estimate=pl.CostEstimate(flops=flops, bytes_accessed=0, transcendentals=0),
        name=name,
    )(*args, *after, *through)


def place():
    blk, swap = lax.axis_index("blk"), lax.axis_index("swap")
    return lax.rem(blk, 2), lax.rem(swap, 2), lax.div(swap, 2)


def quarters():
    core, y, _ = place()
    return [2 * core + y, 2 * (1 - core) + y, 2 * core + 1 - y, 2 * (1 - core) + 1 - y]


def split_kernel(groups, a_ref, b_ref, *rest):
    outs, sems = rest[:-1], rest[-1]
    width = a_ref.shape[1] // 4
    numbers = quarters()
    copies = []
    for group, out in zip(groups, outs):
        for i, member in enumerate(group(numbers)):
            columns = pl.ds(pl.multiple_of(member * width, 128), width)
            for j, src in enumerate((a_ref, b_ref)):
                dst = out.at[:, (2 * i + j) * width : (2 * i + j + 1) * width]
                copies.append(pltpu.make_async_copy(src.at[:, columns], dst, sems.at[len(copies)]))
    for copy in copies:
        copy.start()
    for copy in copies:
        copy.wait()


def choose_kernel(mine, got, *outs):
    core, y, _ = place()
    width = mine.shape[1] // 2
    for odd, (keep, send) in zip((1, 0), (outs[:2], outs[2:])):
        for out, yy in ((keep, y), (send, 1 - y)):
            columns = pl.ds(pl.multiple_of(yy * width, 128), width)

            @pl.when(core == odd)
            def _(out=out, columns=columns):
                out[...] = mine[:, columns]

            @pl.when(core != odd)
            def _(out=out, columns=columns):
                out[...] = got[:, columns]


def select_chunks(blocks, own, by_core, by_y, by_diag):
    core, y, _ = place()
    rows = own.shape[0]
    here = pl.ds(pl.multiple_of(y * rows, rows), rows)
    there = pl.ds(pl.multiple_of((1 - y) * rows, rows), rows)
    for c in (0, 1):

        @pl.when(core == c)
        def _(c=c):
            blocks[c][here, :] = own[...]
            blocks[c][there, :] = by_y[...]
            blocks[1 - c][here, :] = by_core[...]
            blocks[1 - c][there, :] = by_diag[...]


def fill_payloads(n_out, up, down, outs):
    _, _, z = place()
    for k, out in enumerate(outs, 1):

        @pl.when(z + k < n_out)
        def _(out=out):
            out[...] = up[...]

        @pl.when(z + k >= n_out)
        def _(out=out):
            out[...] = down[...]


def payload_kernel(n_out, own, by_core, by_y, by_diag, even, odd, pieces, *outs):
    select_chunks((even, odd), own, by_core, by_y, by_diag)
    _, _, z = place()
    rows = even.shape[0]
    for other in range(n_out):
        where = slice(other * rows, (other + 1) * rows)

        @pl.when(other > z)
        def _(where=where):
            pieces[where, :] = odd[...]

        @pl.when(other <= z)
        def _(where=where):
            pieces[where, :] = even[...]

    fill_payloads(n_out, even, odd, outs)


def attend_kernel(odd, n_out, n_slots, seq_blk, n_given, keep, by_y, starts, doc_scalars, *rest):
    given, rest = rest[:n_given], rest[n_given:]
    if not odd:
        dq_other, rest = rest[0], rest[1:]
    dq_keep, dq_send, rest = rest[0], rest[1], rest[2:]
    sums, rest = rest[:n_slots], rest[n_slots:]
    q_rows, g_rows, keys, vals, scores, dweights, dq_cols, acc, stats, dq_both = rest
    _, y, z = place()
    tok = keep.shape[0]
    width = keep.shape[1] // 2
    heads = width // HEAD_DIM
    pair = 2 * tok
    window = (n_slots - 1) * pair
    inv_root = 1.0 / math.sqrt(HEAD_DIM)
    scale = inv_root * LOG2E
    block = 2 * lax.div(lax.axis_index("blk"), 2) + odd
    first = block * seq_blk + z * pair
    base = first - window
    step_cols = 2 * tok
    n_steps = 2 * width // step_cols

    def stack(unit, src):
        for h in range(heads):
            rows = pl.ds(pl.multiple_of(unit * width + h * tok, tok), tok)
            q_rows[rows, :HEAD_DIM] = src[:, h * HEAD_DIM : (h + 1) * HEAD_DIM]
            g_rows[rows, :] = src[:, width + h * HEAD_DIM : width + (h + 1) * HEAD_DIM]

    stack(y, keep)
    stack(1 - y, by_y)
    unity = (
        lax.broadcasted_iota(jnp.int32, (tok, tok), 0) == lax.broadcasted_iota(jnp.int32, (tok, tok), 1)
    )
    unity = jnp.where(unity, 1.0, 0.0).astype(BF16)
    for h in range(2 * heads):
        rows = slice(h * tok, (h + 1) * tok)
        q_rows[rows, HEAD_DIM:] = unity
    for i in range(n_slots):
        rows = slice(i * pair, (i + 1) * pair)
        back = n_slots - 1 - i
        if n_given == n_slots:
            slot = given[i][...]
        elif back == 0:
            slot = given[2][...]
        elif back == n_out:
            slot = given[1][...]
        else:
            source = lax.rem(z + n_out - back, n_out)
            slot = given[0][pl.ds(pl.multiple_of(source * pair, pair), pair), :]
        for unit in (0, 1):
            keys[unit, rows, :HEAD_DIM] = slot[:, :HEAD_DIM]
        vals[rows, :] = slot[:, HEAD_DIM:]

    begin = lax.div(doc_scalars[first] - base, pair)
    begin_last = lax.div(doc_scalars[first + tok] - base, pair)

    def rows_of(j, count):
        return pl.ds(pl.multiple_of(j * pair, pair), count * pair)

    def cols_of(n):
        return slice(n * step_cols, (n + 1) * step_cols)

    def unit_of(n):
        return n * step_cols // width

    def fold(op, x):
        return op(x.reshape(x.shape[0] // 8, 8, x.shape[1]), axis=0)

    stats[0] = jnp.full(stats.shape[1:], -3e38, F32)
    stats[1] = jnp.zeros(stats.shape[1:], F32)
    stats[2] = jnp.zeros(stats.shape[1:], F32)
    dq_cols[...] = jnp.zeros_like(dq_cols)
    t = lax.broadcasted_iota(jnp.int32, (1, tok), 1)
    lows = [starts[pl.ds(lax.div(first, 128) + unit, 1), :] for unit in (0, 1)]

    def columns_of(units):
        return [n for n in range(n_steps) if unit_of(n) in units]

    def over_slots(step):
        def run(units, start, stop, sizes):
            for size, larger in zip(sizes, (*sizes[1:], None)):
                left = stop - start
                steps = lax.div(left if larger is None else lax.rem(left, larger), size)
                lax.fori_loop(0, steps, lambda i, c: step(units, size, start + size * i, c), 0)
                start = start + size * steps

        run((0,), begin, begin_last, (1, 2))
        run((0, 1), begin_last, n_slots, (1, 2))

    def score_step(units, count, j, carry):
        rows = rows_of(j, count)
        place_j = lax.broadcasted_iota(jnp.int32, (count * pair, tok), 0) + (base + j * pair)
        for unit in units:
            allowed = (place_j >= lows[unit]) & (place_j <= t + (first + unit * tok))
            keys[unit, rows, HEAD_DIM:] = jnp.where(allowed, 0.0, -1e30).astype(BF16)
        for n in columns_of(units):
            s = dot(keys[unit_of(n), rows, :], q_rows[cols_of(n), :], NT)
            scores[rows, cols_of(n)] = s
            stats[0, :, cols_of(n)] = jnp.maximum(stats[0, :, cols_of(n)], fold(jnp.max, s))
        return carry

    over_slots(score_step)
    for n in range(n_steps):
        top = jnp.max(stats[0, :, cols_of(n)], axis=0, keepdims=True)
        stats[0, :, cols_of(n)] = jnp.broadcast_to(top, (8, step_cols))

    def weight_step(units, count, j, carry):
        rows = rows_of(j, count)
        for n in columns_of(units):
            p = jnp.exp2((scores[rows, cols_of(n)] - stats[0, 0:1, cols_of(n)]) * scale)
            scores[rows, cols_of(n)] = p
            stats[1, :, cols_of(n)] += fold(jnp.sum, p)
            dweights[rows, cols_of(n)] = dot(vals[rows, :], g_rows[cols_of(n), :], NT)
        return carry

    over_slots(weight_step)
    for n in range(n_steps):
        inv = 1.0 / jnp.sum(stats[1, :, cols_of(n)], axis=0, keepdims=True)
        stats[1, :, cols_of(n)] = jnp.broadcast_to(inv, (8, step_cols))

    def value_step(units, count, j, carry):
        rows = rows_of(j, count)
        total = jnp.zeros((count * pair, HEAD_DIM), F32)
        for n in columns_of(units):
            d = dweights[rows, cols_of(n)]
            w = scores[rows, cols_of(n)] * stats[1, 0:1, cols_of(n)]
            wb = w.astype(BF16)
            total = total + dot(wb, g_rows[cols_of(n), :], NN)
            scores[rows, cols_of(n)] = w
            stats[2, :, cols_of(n)] += fold(jnp.sum, wb.astype(F32) * d)
        acc[rows, HEAD_DIM:] = total
        return carry

    over_slots(value_step)
    for n in range(n_steps):
        rowdot = jnp.sum(stats[2, :, cols_of(n)], axis=0, keepdims=True)
        stats[2, :, cols_of(n)] = jnp.broadcast_to(rowdot, (8, step_cols))

    def grad_step(units, count, j, carry):
        rows = rows_of(j, count)
        total = jnp.zeros((count * pair, HEAD_DIM), F32)
        k_cols = keys[0, rows, :HEAD_DIM].T
        for n in columns_of(units):
            rest = dweights[rows, cols_of(n)] - stats[2, 0:1, cols_of(n)]
            ds = (scores[rows, cols_of(n)] * rest).astype(BF16)
            total = total + dot(ds, q_rows[cols_of(n), :HEAD_DIM], NN)
            dq_cols[:, cols_of(n)] += dot(k_cols, ds, NN)
        acc[rows, :HEAD_DIM] = total * inv_root
        return carry

    over_slots(grad_step)

    for h in range(2 * heads):
        unit, head = h // heads, h % heads
        dq = (dq_cols[:, h * tok : (h + 1) * tok] * inv_root).T
        dq_both[unit, :, head * HEAD_DIM : (head + 1) * HEAD_DIM] = dq.astype(BF16)
    dq_keep[...] = dq_both[y]
    dq_send[:tok, :] = dq_both[1 - y]
    if not odd:
        dq_send[tok:, :] = dq_other[...]

    for i, out in enumerate(sums):

        @pl.when(i >= begin)
        def _(i=i, out=out):
            out[...] = acc[i * pair : (i + 1) * pair, :].astype(out.dtype)

        @pl.when(i < begin)
        def _(out=out):
            out[...] = jnp.zeros_like(out)


def swapped(parts):
    return [*parts[1:2], *parts[:1], *parts[2:]]


def add_terms(n_out, up, down, terms):
    _, _, z = place()
    for k, term in enumerate(terms, 1):
        value = term[...].astype(F32)
        wrapped = (z + k >= n_out).astype(F32)
        up = up + value * (1.0 - wrapped)
        down = down + value * wrapped
    return up, down


def odd_sum_kernel(n_out, n_terms, own_odd, *refs):
    terms, own_even, (odd_out, even_out) = swapped(refs[:n_terms]), refs[n_terms:-2], refs[-2:]
    even = own_even[0][...] if own_even else jnp.zeros(even_out.shape, F32)
    odd_out[...], even_out[...] = add_terms(n_out, own_odd[...], even, terms)


def home_kernel(n_out, n_terms, own_even, odd_total, even_total, *refs):
    outs, total = refs[-5:-1], refs[-1]
    rim, terms = refs[: -5 - n_terms], refs[-5 - n_terms : -5]
    terms = swapped(terms)
    tok = own_even.shape[0] // 2
    odd = odd_total[...]
    if rim:
        odd = odd + rim[0][...].astype(F32)
    total[0], total[1] = add_terms(n_out, own_even[...] + even_total[...], odd, terms)
    core, y, _ = place()
    for out, c, yy in zip(outs, (core, 1 - core, core, 1 - core), (y, y, 1 - y, 1 - y)):
        out[...] = total[c, pl.ds(pl.multiple_of(yy * tok, tok), tok), :].astype(out.dtype)


def cross_kernel(odd_keep, even_keep, got_ref, out):
    core, y, _ = place()
    tok, width = odd_keep.shape
    even_got, odd_got = got_ref.at[:tok, :], got_ref.at[tok:, :]
    for c, keep, got in ((0, odd_keep, odd_got), (1, even_keep, even_got)):

        @pl.when(core == c)
        def _(keep=keep, got=got):
            out[:, pl.ds(pl.multiple_of(y * width, 128), width)] = keep[...]
            out[:, pl.ds(pl.multiple_of((1 - y) * width, 128), width)] = got[...]


def finish_kernel(odd_keep, even_keep, got_ref, crossed, *refs):
    parts, (out, k_out, v_out) = refs[:4], refs[4:]
    core, y, _ = place()
    tok, width = odd_keep.shape
    even_got, odd_got = got_ref.at[:tok, :], got_ref.at[tok:, :]

    def columns(quarter, count=1, size=width):
        return pl.ds(pl.multiple_of(quarter * size, 128), count * size)

    for c, keep, got in ((0, even_keep, even_got), (1, odd_keep, odd_got)):

        @pl.when(core == c)
        def _(keep=keep, got=got):
            out[:, columns(2 * core + y)] = keep[...]
            out[:, columns(2 * core + 1 - y)] = got[...]

    out[:, columns(2 * (1 - core), 2)] = crossed[...]
    kv_width = parts[0].shape[1] // 2
    for quarter, part in zip(quarters(), parts):
        k_out[:, columns(quarter, 1, kv_width)] = part[:, :kv_width].astype(BF16)
        v_out[:, columns(quarter, 1, kv_width)] = part[:, kv_width:].astype(BF16)


def body(queries, keys, values, grad_out, doc_ids):
    tok = queries.shape[0]
    n_blk, n_swap = lax.axis_size("blk"), lax.axis_size("swap")
    n_out = n_swap // 2
    seq_blk = tok * n_swap
    pair = 2 * tok
    far = -(-MOST // pair)
    q_width, kv_width = queries.shape[1] // 4, keys.shape[1] // 4
    both = ("swap", "blk")
    devices = [(b, s) for b in range(n_blk) for s in range(n_swap)]

    def index(b, s):
        return s * n_blk + b

    routes = [
        [(index(b, s), index(b ^ 1, s)) for b, s in devices],
        [(index(b, s), index(b, s ^ 1)) for b, s in devices],
        [(index(b, s), index(b ^ 1, s ^ 1)) for b, s in devices],
    ]

    def to_partners(parts):
        return [lax.ppermute(part, both, route) for part, route in zip(parts, routes)]

    def odd_route(k):
        return [(index(b, s), index(b, 2 * ((s // 2 + k) % n_out) + s % 2)) for b, s in devices]

    def even_route(k):
        route = []
        for b, s in devices:
            step, z = divmod(s // 2 + k, n_out)
            if b + 2 * step < n_blk:
                route.append((index(b, s), index(b + 2 * step, 2 * z + s % 2)))
        return route

    def along_z(parts, route_of, back=False):
        got = []
        for k, part in zip(shifts, parts):
            route = route_of(k)
            got.append(lax.ppermute(part, both, [(b, a) for a, b in route] if back else route))
        return got

    def gathered(pieces):
        groups = [[2 * z + y for z in range(n_out)] for y in (0, 1)]
        got = lax.all_to_all(
            pieces.reshape(n_out, pair, -1), "swap", 0, 0, axis_index_groups=groups
        )
        return got.reshape(pieces.shape)

    def along_x(part, step):
        return lax.ppermute(
            part, "blk", [(b, b + step) for b in range(n_blk) if 0 <= b + step < n_blk]
        )

    def shape(rows, cols, dtype=BF16):
        return jax.ShapeDtypeStruct((rows, cols), dtype)

    def split(a, b, width, groups, name, after=()):
        return vmem_call(
            functools.partial(split_kernel, groups),
            [shape(tok, 8 * width // len(groups))] * len(groups),
            (a, b),
            scratch=[pltpu.SemaphoreType.DMA((8,))],
            hbm=(0, 1),
            after=after,
            name=name,
        )

    shifts = [k for k in range(1, far + 1) if k < n_out]
    whole_ring = far == n_out
    block_shape = shape(pair, 2 * kv_width)
    sum_shape = shape(pair, 2 * kv_width, F32)

    one_each = [lambda numbers, i=i: [numbers[i]] for i in range(4)]
    by_core = [lambda numbers: [numbers[0] // 2 * 2 + i for i in (0, 1)], lambda numbers: [numbers[1] // 2 * 2 + i for i in (0, 1)]]
    kv_parts = [
        jnp.concatenate(
            [lax.dynamic_slice_in_dim(x, quarter * kv_width, kv_width, 1) for x in (keys, values)], 1
        )
        for quarter in quarters()
    ]
    kv_recv = to_partners(kv_parts[1:])
    half = 2 * q_width

    def halves(which):
        parts = [lax.dynamic_slice_in_dim(x, which * half, half, 1) for x in (queries, grad_out)]
        return jnp.concatenate(
            [x[:, i * q_width : (i + 1) * q_width] for i in (0, 1) for x in parts], 1
        )

    core = place()[0]
    mine, other = halves(core), halves(1 - core)
    *made, other = vmem_call(
        functools.partial(payload_kernel, n_out),
        [block_shape] * 2 + [shape(n_out * pair, 2 * kv_width)] + [block_shape] * len(shifts),
        (kv_parts[0], *kv_recv),
        through=(other,),
        name="payload",
    )
    crossed = lax.ppermute(other, both, routes[0])
    odd_qg, odd_send, even_qg, even_send = vmem_call(
        choose_kernel, [shape(tok, 2 * q_width)] * 4, (mine, crossed), after=(made[0],), name="choose_qg"
    )
    even, odd, odd_pieces, *pays = made
    odd_got = gathered(odd_pieces)
    odd_qg = (odd_qg, lax.ppermute(odd_send, both, routes[1]))
    even_got = along_z(pays, even_route)
    even_qg = (even_qg, lax.ppermute(even_send, both, routes[1]))
    rim = along_x(odd, 2) if whole_ring else None

    starts = doc_ids.reshape(-1, 128)
    n_slots = far + 1
    rows = 2 * (q_width // HEAD_DIM) * tok
    sum_shapes = [
        sum_shape if i == far or (i == 0 and whole_ring and which) else block_shape
        for which in (0, 1)
        for i in range(n_slots)
    ]

    def attend(which, slots, qg, dq_other=None):
        return vmem_call(
            functools.partial(attend_kernel, which, n_out, n_slots, seq_blk, len(slots)),
            [shape(tok, q_width), shape(tok if which else pair, q_width)]
            + sum_shapes[which * n_slots : (which + 1) * n_slots],
            (*qg, starts, doc_ids, *slots) + (() if which else (dq_other,)),
            scratch=[
                pltpu.VMEM((rows, 2 * HEAD_DIM), BF16),
                pltpu.VMEM((rows, HEAD_DIM), BF16),
                pltpu.VMEM((2, n_slots * pair, 2 * HEAD_DIM), BF16),
                pltpu.VMEM((n_slots * pair, HEAD_DIM), BF16),
                pltpu.VMEM((n_slots * pair, rows), F32),
                pltpu.VMEM((n_slots * pair, rows), F32),
                pltpu.VMEM((HEAD_DIM, rows), F32),
                pltpu.VMEM((n_slots * pair, 2 * HEAD_DIM), F32),
                pltpu.VMEM((3, 8, rows), F32),
                pltpu.VMEM((2, tok, q_width), BF16),
            ],
            smem=(3,),
            mib=28,
            flops=6_000_000_000,
            name="attend_odd" if which else "attend_even",
        )

    def slots_of(up, down, got):
        return [down if k == n_out else got[k - 1] for k in range(far, 0, -1)] + [up]

    def sent(sums):
        return [sums[far - k] for k in shifts]

    dq_odd, dq_odd_send, *odd_sums = attend(1, (odd_got, even, odd), odd_qg)
    odd_back = along_z(sent(odd_sums), odd_route, back=True)
    dq_even, dq_send, *even_sums = attend(0, slots_of(even, rim, even_got), even_qg, dq_odd_send)
    odd_total, even_total, dq_send, *even_sent = vmem_call(
        functools.partial(odd_sum_kernel, n_out, len(shifts)),
        [sum_shape, sum_shape],
        (odd_sums[far], *swapped(odd_back), *([odd_sums[0]] if whole_ring else [])),
        through=[dq_send, *sent(even_sums)],
        name="odd_sum",
    )
    dq_got = lax.ppermute(dq_send, both, routes[1])
    rim_home = (along_x(even_sums[0], -2),) if whole_ring else ()
    even_back = along_z(even_sent, even_route, back=True)
    home = vmem_call(
        functools.partial(home_kernel, n_out, len(shifts)),
        [shape(tok, 2 * kv_width, F32)] + [shape(tok, 2 * kv_width)] * 3,
        (even_sums[far], odd_total, even_total, *rim_home, *swapped(even_back)),
        scratch=[pltpu.VMEM((2, pair, 2 * kv_width), F32)],
        name="home",
    )
    kv_home = to_partners(home[1:])
    dq_parts = (dq_odd, dq_even, dq_got)
    (dq_cross,) = vmem_call(cross_kernel, [shape(tok, 2 * q_width)], dq_parts, after=(home[0],), name="cross")
    return vmem_call(
        finish_kernel,
        [shape(*queries.shape), shape(*keys.shape), shape(*values.shape)],
        (*dq_parts, lax.ppermute(dq_cross, both, routes[0]), home[0], *kv_home),
        name="finish",
    )


def solution(mesh):
    spec = P(("blk", "swap"), None)
    return jax.shard_map(
        lambda *args: tuple(body(*args)),
        mesh=mesh,
        in_specs=(spec, spec, spec, spec, P()),
        out_specs=(spec, spec, spec),
        check_vma=False,
    )
```

```python
import functools
import math

import jax
import jax.numpy as jnp
from jax import lax
from jax.experimental import pallas as pl
from jax.experimental.pallas import tpu as pltpu
from jax.sharding import PartitionSpec as P

HEAD_DIM = 128
MOST = 1024
BF16 = jnp.bfloat16
F32 = jnp.float32
LOG2E = 1.4426950408889634
MIB = 1024 * 1024

NN = (((1,), (0,)), ((), ()))
NT = (((1,), (1,)), ((), ()))
TN = (((0,), (0,)), ((), ()))


def dot(a, b, dims):
    return lax.dot_general(a, b, dims, preferred_element_type=F32)


def vmem_call(kernel, out_shapes, args, scratch=(), hbm=(), smem=(), after=(), through=(), mib=4, flops=0, name=None):
    def space(i):
        return pltpu.SMEM if i in smem else pltpu.HBM if i in hbm else pltpu.VMEM

    specs = [pl.BlockSpec(memory_space=space(i)) for i in range(len(args))]
    specs += [pl.BlockSpec(memory_space=pl.ANY)] * (len(after) + len(through))
    outs = [pl.BlockSpec(memory_space=pltpu.VMEM)] * len(out_shapes)
    outs += [pl.BlockSpec(memory_space=pl.ANY)] * len(through)
    n_args, n_out = len(args), len(out_shapes)
    n_in, n_made = len(specs), len(outs)

    def run(*refs):
        kernel(*refs[:n_args], *refs[n_in : n_in + n_out], *refs[n_in + n_made :])

    return pl.pallas_call(
        run,
        out_shape=list(out_shapes) + [jax.ShapeDtypeStruct(t.shape, t.dtype) for t in through],
        in_specs=specs,
        out_specs=outs,
        input_output_aliases={n_args + len(after) + i: n_out + i for i in range(len(through))},
        scratch_shapes=list(scratch),
        compiler_params=pltpu.CompilerParams(vmem_limit_bytes=mib * MIB),
        cost_estimate=pl.CostEstimate(flops=flops, bytes_accessed=0, transcendentals=0),
        name=name,
    )(*args, *after, *through)


def place():
    blk, swap = lax.axis_index("blk"), lax.axis_index("swap")
    return lax.rem(blk, 2), lax.rem(swap, 2), lax.div(swap, 2)


def quarters():
    core, y, _ = place()
    return [2 * core + y, 2 * (1 - core) + y, 2 * core + 1 - y, 2 * (1 - core) + 1 - y]


def split_kernel(groups, a_ref, b_ref, *rest):
    outs, sems = rest[:-1], rest[-1]
    width = a_ref.shape[1] // 4
    numbers = quarters()
    copies = []
    for group, out in zip(groups, outs):
        for i, member in enumerate(group(numbers)):
            columns = pl.ds(pl.multiple_of(member * width, 128), width)
            for j, src in enumerate((a_ref, b_ref)):
                dst = out.at[:, (2 * i + j) * width : (2 * i + j + 1) * width]
                copies.append(pltpu.make_async_copy(src.at[:, columns], dst, sems.at[len(copies)]))
    for copy in copies:
        copy.start()
    for copy in copies:
        copy.wait()


def choose_kernel(mine, got, *outs):
    core, y, _ = place()
    width = mine.shape[1] // 2
    for odd, (keep, send) in zip((1, 0), (outs[:2], outs[2:])):
        for out, yy in ((keep, y), (send, 1 - y)):
            columns = pl.ds(pl.multiple_of(yy * width, 128), width)

            @pl.when(core == odd)
            def _(out=out, columns=columns):
                out[...] = mine[:, columns]

            @pl.when(core != odd)
            def _(out=out, columns=columns):
                out[...] = got[:, columns]


def select_chunks(blocks, own, by_core, by_y, by_diag):
    core, y, _ = place()
    rows = own.shape[0]
    here = pl.ds(pl.multiple_of(y * rows, rows), rows)
    there = pl.ds(pl.multiple_of((1 - y) * rows, rows), rows)
    for c in (0, 1):

        @pl.when(core == c)
        def _(c=c):
            blocks[c][here, :] = own[...]
            blocks[c][there, :] = by_y[...]
            blocks[1 - c][here, :] = by_core[...]
            blocks[1 - c][there, :] = by_diag[...]


def fill_payloads(n_out, up, down, outs):
    _, _, z = place()
    for k, out in enumerate(outs, 1):

        @pl.when(z + k < n_out)
        def _(out=out):
            out[...] = up[...]

        @pl.when(z + k >= n_out)
        def _(out=out):
            out[...] = down[...]


def payload_kernel(n_out, own, by_core, by_y, by_diag, even, odd, pieces, *outs):
    select_chunks((even, odd), own, by_core, by_y, by_diag)
    _, _, z = place()
    rows = even.shape[0]
    for other in range(n_out):
        where = slice(other * rows, (other + 1) * rows)

        @pl.when(other > z)
        def _(where=where):
            pieces[where, :] = odd[...]

        @pl.when(other <= z)
        def _(where=where):
            pieces[where, :] = even[...]

    fill_payloads(n_out, even, odd, outs)


def attend_kernel(odd, n_out, n_slots, seq_blk, n_given, keep, by_y, starts, doc_scalars, *rest):
    given, rest = rest[:n_given], rest[n_given:]
    if not odd:
        dq_other, rest = rest[0], rest[1:]
    dq_keep, dq_send, rest = rest[0], rest[1], rest[2:]
    sums, rest = rest[:n_slots], rest[n_slots:]
    q_rows, g_rows, keys, vals, scores, dweights, dq_cols, acc, stats, dq_both = rest
    _, y, z = place()
    tok = keep.shape[0]
    width = keep.shape[1] // 2
    heads = width // HEAD_DIM
    pair = 2 * tok
    window = (n_slots - 1) * pair
    inv_root = 1.0 / math.sqrt(HEAD_DIM)
    scale = inv_root * LOG2E
    block = 2 * lax.div(lax.axis_index("blk"), 2) + odd
    first = block * seq_blk + z * pair
    base = first - window
    step_cols = 2 * tok
    n_steps = 2 * width // step_cols

    def stack(unit, src):
        for h in range(heads):
            rows = pl.ds(pl.multiple_of(unit * width + h * tok, tok), tok)
            q_rows[rows, :HEAD_DIM] = src[:, h * HEAD_DIM : (h + 1) * HEAD_DIM]
            g_rows[rows, :] = src[:, width + h * HEAD_DIM : width + (h + 1) * HEAD_DIM]

    stack(y, keep)
    stack(1 - y, by_y)
    unity = (
        lax.broadcasted_iota(jnp.int32, (tok, tok), 0) == lax.broadcasted_iota(jnp.int32, (tok, tok), 1)
    )
    unity = jnp.where(unity, 1.0, 0.0).astype(BF16)
    for h in range(2 * heads):
        rows = slice(h * tok, (h + 1) * tok)
        q_rows[rows, HEAD_DIM:] = unity
    for i in range(n_slots):
        rows = slice(i * pair, (i + 1) * pair)
        back = n_slots - 1 - i
        if n_given == n_slots:
            slot = given[i][...]
        elif back == 0:
            slot = given[2][...]
        elif back == n_out:
            slot = given[1][...]
        else:
            source = lax.rem(z + n_out - back, n_out)
            slot = given[0][pl.ds(pl.multiple_of(source * pair, pair), pair), :]
        for unit in (0, 1):
            keys[unit, rows, :HEAD_DIM] = slot[:, :HEAD_DIM]
        vals[rows, :] = slot[:, HEAD_DIM:]

    begin = lax.div(doc_scalars[first] - base, pair)
    begin_last = lax.div(doc_scalars[first + tok] - base, pair)

    def rows_of(j, count):
        return pl.ds(pl.multiple_of(j * pair, pair), count * pair)

    def cols_of(n):
        return slice(n * step_cols, (n + 1) * step_cols)

    def unit_of(n):
        return n * step_cols // width

    def fold(op, x):
        return op(x.reshape(x.shape[0] // 8, 8, x.shape[1]), axis=0)

    stats[0] = jnp.full(stats.shape[1:], -3e38, F32)
    stats[1] = jnp.zeros(stats.shape[1:], F32)
    stats[2] = jnp.zeros(stats.shape[1:], F32)
    dq_cols[...] = jnp.zeros_like(dq_cols)
    t = lax.broadcasted_iota(jnp.int32, (1, tok), 1)
    lows = [starts[pl.ds(lax.div(first, 128) + unit, 1), :] for unit in (0, 1)]

    def columns_of(units):
        return [n for n in range(n_steps) if unit_of(n) in units]

    def over_slots(step):
        def run(units, start, stop, sizes):
            for size, larger in zip(sizes, (*sizes[1:], None)):
                left = stop - start
                steps = lax.div(left if larger is None else lax.rem(left, larger), size)
                lax.fori_loop(0, steps, lambda i, c: step(units, size, start + size * i, c), 0)
                start = start + size * steps

        run((0,), begin, begin_last, (1, 2))
        run((0, 1), begin_last, n_slots, (1, 2))

    def score_step(units, count, j, carry):
        rows = rows_of(j, count)
        place_j = lax.broadcasted_iota(jnp.int32, (count * pair, tok), 0) + (base + j * pair)
        for unit in units:
            allowed = (place_j >= lows[unit]) & (place_j <= t + (first + unit * tok))
            keys[unit, rows, HEAD_DIM:] = jnp.where(allowed, 0.0, -1e30).astype(BF16)
        for n in columns_of(units):
            s = dot(keys[unit_of(n), rows, :], q_rows[cols_of(n), :], NT)
            scores[rows, cols_of(n)] = s
            stats[0, :, cols_of(n)] = jnp.maximum(stats[0, :, cols_of(n)], fold(jnp.max, s))
        return carry

    over_slots(score_step)
    for n in range(n_steps):
        top = jnp.max(stats[0, :, cols_of(n)], axis=0, keepdims=True)
        stats[0, :, cols_of(n)] = jnp.broadcast_to(top, (8, step_cols))

    def weight_step(units, count, j, carry):
        rows = rows_of(j, count)
        for n in columns_of(units):
            p = jnp.exp2((scores[rows, cols_of(n)] - stats[0, 0:1, cols_of(n)]) * scale)
            scores[rows, cols_of(n)] = p
            stats[1, :, cols_of(n)] += fold(jnp.sum, p)
            dweights[rows, cols_of(n)] = dot(vals[rows, :], g_rows[cols_of(n), :], NT)
        return carry

    over_slots(weight_step)
    for n in range(n_steps):
        inv = 1.0 / jnp.sum(stats[1, :, cols_of(n)], axis=0, keepdims=True)
        stats[1, :, cols_of(n)] = jnp.broadcast_to(inv, (8, step_cols))

    def value_step(units, count, j, carry):
        rows = rows_of(j, count)
        total = jnp.zeros((count * pair, HEAD_DIM), F32)
        for n in columns_of(units):
            d = dweights[rows, cols_of(n)]
            w = scores[rows, cols_of(n)] * stats[1, 0:1, cols_of(n)]
            wb = w.astype(BF16)
            total = total + dot(wb, g_rows[cols_of(n), :], NN)
            scores[rows, cols_of(n)] = w
            stats[2, :, cols_of(n)] += fold(jnp.sum, wb.astype(F32) * d)
        acc[rows, HEAD_DIM:] = total
        return carry

    over_slots(value_step)
    for n in range(n_steps):
        rowdot = jnp.sum(stats[2, :, cols_of(n)], axis=0, keepdims=True)
        stats[2, :, cols_of(n)] = jnp.broadcast_to(rowdot, (8, step_cols))

    def grad_step(units, count, j, carry):
        rows = rows_of(j, count)
        total = jnp.zeros((count * pair, HEAD_DIM), F32)
        k_cols = keys[0, rows, :HEAD_DIM].T
        for n in columns_of(units):
            rest = dweights[rows, cols_of(n)] - stats[2, 0:1, cols_of(n)]
            ds = (scores[rows, cols_of(n)] * rest).astype(BF16)
            total = total + dot(ds, q_rows[cols_of(n), :HEAD_DIM], NN)
            dq_cols[:, cols_of(n)] += dot(k_cols, ds, NN)
        acc[rows, :HEAD_DIM] = total * inv_root
        return carry

    over_slots(grad_step)

    for h in range(2 * heads):
        unit, head = h // heads, h % heads
        dq = (dq_cols[:, h * tok : (h + 1) * tok] * inv_root).astype(BF16).T
        dq_both[unit, :, head * HEAD_DIM : (head + 1) * HEAD_DIM] = dq
    dq_keep[...] = dq_both[y]
    dq_send[:tok, :] = dq_both[1 - y]
    if not odd:
        dq_send[tok:, :] = dq_other[...]

    for i, out in enumerate(sums):

        @pl.when(i >= begin)
        def _(i=i, out=out):
            out[...] = acc[i * pair : (i + 1) * pair, :].astype(out.dtype)

        @pl.when(i < begin)
        def _(out=out):
            out[...] = jnp.zeros_like(out)


def swapped(parts):
    return [*parts[1:2], *parts[:1], *parts[2:]]


def add_terms(n_out, up, down, terms):
    _, _, z = place()
    for k, term in enumerate(terms, 1):
        value = term[...].astype(F32)
        wrapped = (z + k >= n_out).astype(F32)
        up = up + value * (1.0 - wrapped)
        down = down + value * wrapped
    return up, down


def odd_sum_kernel(n_out, n_terms, own_odd, *refs):
    terms, own_even, (odd_out, even_out) = swapped(refs[:n_terms]), refs[n_terms:-2], refs[-2:]
    even = own_even[0][...] if own_even else jnp.zeros(even_out.shape, F32)
    odd_out[...], even_out[...] = add_terms(n_out, own_odd[...], even, terms)


def home_kernel(n_out, n_terms, own_even, odd_total, even_total, *refs):
    outs, total = refs[-5:-1], refs[-1]
    rim, terms = refs[: -5 - n_terms], refs[-5 - n_terms : -5]
    terms = swapped(terms)
    tok = own_even.shape[0] // 2
    odd = odd_total[...]
    if rim:
        odd = odd + rim[0][...].astype(F32)
    total[0], total[1] = add_terms(n_out, own_even[...] + even_total[...], odd, terms)
    core, y, _ = place()
    for out, c, yy in zip(outs, (core, 1 - core, core, 1 - core), (y, y, 1 - y, 1 - y)):
        out[...] = total[c, pl.ds(pl.multiple_of(yy * tok, tok), tok), :].astype(out.dtype)


def cross_kernel(odd_keep, even_keep, got_ref, out):
    core, y, _ = place()
    tok, width = odd_keep.shape
    even_got, odd_got = got_ref.at[:tok, :], got_ref.at[tok:, :]
    for c, keep, got in ((0, odd_keep, odd_got), (1, even_keep, even_got)):

        @pl.when(core == c)
        def _(keep=keep, got=got):
            out[:, pl.ds(pl.multiple_of(y * width, 128), width)] = keep[...]
            out[:, pl.ds(pl.multiple_of((1 - y) * width, 128), width)] = got[...]


def finish_kernel(odd_keep, even_keep, got_ref, crossed, *refs):
    parts, (out, k_out, v_out) = refs[:4], refs[4:]
    core, y, _ = place()
    tok, width = odd_keep.shape
    even_got, odd_got = got_ref.at[:tok, :], got_ref.at[tok:, :]

    def columns(quarter, count=1, size=width):
        return pl.ds(pl.multiple_of(quarter * size, 128), count * size)

    for c, keep, got in ((0, even_keep, even_got), (1, odd_keep, odd_got)):

        @pl.when(core == c)
        def _(keep=keep, got=got):
            out[:, columns(2 * core + y)] = keep[...]
            out[:, columns(2 * core + 1 - y)] = got[...]

    out[:, columns(2 * (1 - core), 2)] = crossed[...]
    kv_width = parts[0].shape[1] // 2
    for quarter, part in zip(quarters(), parts):
        k_out[:, columns(quarter, 1, kv_width)] = part[:, :kv_width].astype(BF16)
        v_out[:, columns(quarter, 1, kv_width)] = part[:, kv_width:].astype(BF16)


def body(queries, keys, values, grad_out, doc_ids):
    tok = queries.shape[0]
    n_blk, n_swap = lax.axis_size("blk"), lax.axis_size("swap")
    n_out = n_swap // 2
    seq_blk = tok * n_swap
    pair = 2 * tok
    far = -(-MOST // pair)
    q_width, kv_width = queries.shape[1] // 4, keys.shape[1] // 4
    both = ("swap", "blk")
    devices = [(b, s) for b in range(n_blk) for s in range(n_swap)]

    def index(b, s):
        return s * n_blk + b

    routes = [
        [(index(b, s), index(b ^ 1, s)) for b, s in devices],
        [(index(b, s), index(b, s ^ 1)) for b, s in devices],
        [(index(b, s), index(b ^ 1, s ^ 1)) for b, s in devices],
    ]

    def to_partners(parts):
        return [lax.ppermute(part, both, route) for part, route in zip(parts, routes)]

    def odd_route(k):
        return [(index(b, s), index(b, 2 * ((s // 2 + k) % n_out) + s % 2)) for b, s in devices]

    def even_route(k):
        route = []
        for b, s in devices:
            step, z = divmod(s // 2 + k, n_out)
            if b + 2 * step < n_blk:
                route.append((index(b, s), index(b + 2 * step, 2 * z + s % 2)))
        return route

    def along_z(parts, route_of, back=False):
        got = []
        for k, part in zip(shifts, parts):
            route = route_of(k)
            got.append(lax.ppermute(part, both, [(b, a) for a, b in route] if back else route))
        return got

    def gathered(pieces):
        groups = [[2 * z + y for z in range(n_out)] for y in (0, 1)]
        got = lax.all_to_all(
            pieces.reshape(n_out, pair, -1), "swap", 0, 0, axis_index_groups=groups
        )
        return got.reshape(pieces.shape)

    def along_x(part, step):
        return lax.ppermute(
            part, "blk", [(b, b + step) for b in range(n_blk) if 0 <= b + step < n_blk]
        )

    def shape(rows, cols, dtype=BF16):
        return jax.ShapeDtypeStruct((rows, cols), dtype)

    def split(a, b, width, groups, name, after=()):
        return vmem_call(
            functools.partial(split_kernel, groups),
            [shape(tok, 8 * width // len(groups))] * len(groups),
            (a, b),
            scratch=[pltpu.SemaphoreType.DMA((8,))],
            hbm=(0, 1),
            after=after,
            name=name,
        )

    shifts = [k for k in range(1, far + 1) if k < n_out]
    whole_ring = far == n_out
    block_shape = shape(pair, 2 * kv_width)
    sum_shape = shape(pair, 2 * kv_width, F32)

    one_each = [lambda numbers, i=i: [numbers[i]] for i in range(4)]
    by_core = [lambda numbers: [numbers[0] // 2 * 2 + i for i in (0, 1)], lambda numbers: [numbers[1] // 2 * 2 + i for i in (0, 1)]]
    kv_parts = [
        jnp.concatenate(
            [lax.dynamic_slice_in_dim(x, quarter * kv_width, kv_width, 1) for x in (keys, values)], 1
        )
        for quarter in quarters()
    ]
    kv_recv = to_partners(kv_parts[1:])
    half = 2 * q_width

    def halves(which):
        parts = [lax.dynamic_slice_in_dim(x, which * half, half, 1) for x in (queries, grad_out)]
        return jnp.concatenate(
            [x[:, i * q_width : (i + 1) * q_width] for i in (0, 1) for x in parts], 1
        )

    core = place()[0]
    mine, other = halves(core), halves(1 - core)
    *made, other = vmem_call(
        functools.partial(payload_kernel, n_out),
        [block_shape] * 2 + [shape(n_out * pair, 2 * kv_width)] + [block_shape] * len(shifts),
        (kv_parts[0], *kv_recv),
        through=(other,),
        name="payload",
    )
    crossed = lax.ppermute(other, both, routes[0])
    odd_qg, odd_send, even_qg, even_send = vmem_call(
        choose_kernel, [shape(tok, 2 * q_width)] * 4, (mine, crossed), after=(made[0],), name="choose_qg"
    )
    even, odd, odd_pieces, *pays = made
    odd_got = gathered(odd_pieces)
    odd_qg = (odd_qg, lax.ppermute(odd_send, both, routes[1]))
    even_got = along_z(pays, even_route)
    even_qg = (even_qg, lax.ppermute(even_send, both, routes[1]))
    rim = along_x(odd, 2) if whole_ring else None

    starts = doc_ids.reshape(-1, 128)
    n_slots = far + 1
    rows = 2 * (q_width // HEAD_DIM) * tok
    sum_shapes = [
        sum_shape if i == far or (i == 0 and whole_ring and which) else block_shape
        for which in (0, 1)
        for i in range(n_slots)
    ]

    def attend(which, slots, qg, dq_other=None):
        return vmem_call(
            functools.partial(attend_kernel, which, n_out, n_slots, seq_blk, len(slots)),
            [shape(tok, q_width), shape(tok if which else pair, q_width)]
            + sum_shapes[which * n_slots : (which + 1) * n_slots],
            (*qg, starts, doc_ids, *slots) + (() if which else (dq_other,)),
            scratch=[
                pltpu.VMEM((rows, 2 * HEAD_DIM), BF16),
                pltpu.VMEM((rows, HEAD_DIM), BF16),
                pltpu.VMEM((2, n_slots * pair, 2 * HEAD_DIM), BF16),
                pltpu.VMEM((n_slots * pair, HEAD_DIM), BF16),
                pltpu.VMEM((n_slots * pair, rows), F32),
                pltpu.VMEM((n_slots * pair, rows), F32),
                pltpu.VMEM((HEAD_DIM, rows), F32),
                pltpu.VMEM((n_slots * pair, 2 * HEAD_DIM), F32),
                pltpu.VMEM((3, 8, rows), F32),
                pltpu.VMEM((2, tok, q_width), BF16),
            ],
            smem=(3,),
            mib=28,
            flops=6_000_000_000,
            name="attend_odd" if which else "attend_even",
        )

    def slots_of(up, down, got):
        return [down if k == n_out else got[k - 1] for k in range(far, 0, -1)] + [up]

    def sent(sums):
        return [sums[far - k] for k in shifts]

    dq_odd, dq_odd_send, *odd_sums = attend(1, (odd_got, even, odd), odd_qg)
    odd_back = along_z(sent(odd_sums), odd_route, back=True)
    dq_even, dq_send, *even_sums = attend(0, slots_of(even, rim, even_got), even_qg, dq_odd_send)
    odd_total, even_total, dq_send, *even_sent = vmem_call(
        functools.partial(odd_sum_kernel, n_out, len(shifts)),
        [sum_shape, sum_shape],
        (odd_sums[far], *swapped(odd_back), *([odd_sums[0]] if whole_ring else [])),
        through=[dq_send, *sent(even_sums)],
        name="odd_sum",
    )
    dq_got = lax.ppermute(dq_send, both, routes[1])
    rim_home = (along_x(even_sums[0], -2),) if whole_ring else ()
    even_back = along_z(even_sent, even_route, back=True)
    home = vmem_call(
        functools.partial(home_kernel, n_out, len(shifts)),
        [shape(tok, 2 * kv_width, F32)] + [shape(tok, 2 * kv_width)] * 3,
        (even_sums[far], odd_total, even_total, *rim_home, *swapped(even_back)),
        scratch=[pltpu.VMEM((2, pair, 2 * kv_width), F32)],
        name="home",
    )
    kv_home = to_partners(home[1:])
    dq_parts = (dq_odd, dq_even, dq_got)
    (dq_cross,) = vmem_call(cross_kernel, [shape(tok, 2 * q_width)], dq_parts, after=(home[0],), name="cross")
    return vmem_call(
        finish_kernel,
        [shape(*queries.shape), shape(*keys.shape), shape(*values.shape)],
        (*dq_parts, lax.ppermute(dq_cross, both, routes[0]), home[0], *kv_home),
        name="finish",
    )


def solution(mesh):
    spec = P(("blk", "swap"), None)
    return jax.shard_map(
        lambda *args: tuple(body(*args)),
        mesh=mesh,
        in_specs=(spec, spec, spec, spec, P()),
        out_specs=(spec, spec, spec),
        check_vma=False,
    )
```
